128 devices in a mesh: lon: 32 (over z, y, core), lat: 4 (over x).
Axes of the slice: x: 4, y: 4, z: 4, core: 2. Of those that a mesh axis runs over, the one named last changes fastest.
Arguments:
- node_latent: bfloat16 [32768, 512], P(('lon', 'lat')), may hold values from -6 to 6
- edge_latent: bfloat16 [262144, 512], P(('lon', 'lat')), may hold values from -6 to 6
- edge_sender: int32 [262144], P(('lon', 'lat')), may hold values from 0 to 511
- edge_receiver: int32 [262144], P(('lon', 'lat')), may hold values from 0 to 255, as said below
- edge_count: int32 [128], P(('lon', 'lat')), may hold values from 256 to 2048, as said below
- halo_send: int32 [128, 4, 64], P(('lon', 'lat')), may hold values from 0 to 255
- weight_in: bfloat16 [1536, 512], replicated, may hold values from -0.15625 to 0.15625
- bias_in: float32 [512], replicated, may hold values from -3 to 3
- weight_out: bfloat16 [512, 512], replicated, may hold values from -0.25 to 0.25
- bias_out: float32 [512], replicated, may hold values from -3 to 3
- norm_gain: float32 [512], replicated, may hold values from 0.5 to 1.5
- edge_cotangent: bfloat16 [262144, 512], P(('lon', 'lat')), may hold values from -6 to 6
- node_cotangent: bfloat16 [32768, 512], P(('lon', 'lat')), may hold values from -6 to 6
Outputs:
- edge_grad: bfloat16 [262144, 512], P(('lon', 'lat'))
- node_grad: bfloat16 [32768, 512], P(('lon', 'lat'))
- grad_w_in: float32 [1536, 512], replicated
- grad_b_in: float32 [512], replicated
- grad_w_out: float32 [512, 512], replicated
- grad_b_out: float32 [512], replicated
- grad_gain: float32 [512], replicated
The draws below stay inside these ranges and needn't reach their ends.
Inputs may be any that keep to these rules, and one draw needn't show every extreme that they name: `edge_receiver`: within each partition's block of 2048 entries the values never fall. `edge_count`: some partition is full in every draw.
All inputs are finite; a program needn't handle non-finite values.
Results may differ from the reference program's by a relative error of at most 0.0047.
Values may be sent and summed in bfloat16 or wider, within the bound.
A program may use at most 128 MiB of HBM per device.

```python
import jax
import jax.numpy as jnp
from jax import lax

D = 512
NODE_DEV = 256
EDGE_DEV = 2048
HALO = 64
NODES = 32768
EDGES = 262144
N_LON = 32
N_LAT = 4


def draw_edge_receiver(key, part):
    key = jax.random.fold_in(key, 7)
    values = jax.random.randint(key, (N_LON * N_LAT, EDGE_DEV), 0, NODE_DEV, dtype=jnp.int32)
    return jnp.sort(values, axis=1).reshape(-1).astype(jnp.int32)


def draw_edge_count(key, part):
    key = jax.random.fold_in(key, 11)
    first, second = jax.random.split(key)
    parts = N_LON * N_LAT
    counts = jax.random.randint(first, (parts,), EDGE_DEV // 8, EDGE_DEV + 1, dtype=jnp.int32)
    chosen = jax.random.randint(second, (), 0, parts, dtype=jnp.int32)
    return jnp.where(jnp.arange(parts, dtype=jnp.int32) == chosen, EDGE_DEV, counts).astype(jnp.int32)


def set_ends(array, key, low, high):
    longest = array.shape.index(max(array.shape))
    spots = []
    for shift in (0, 1):
        where = [jax.random.randint(jax.random.fold_in(key, axis), (), 0, length) for axis, length in enumerate(array.shape)]
        where[longest] = (where[longest] + shift) % array.shape[longest]
        spots.append(tuple(where))
    return array.at[spots[0]].set(low).at[spots[1]].set(high)


def block_levels(key, shape, pieces, low, top_value):
    gain = 1.0
    for position, shards_of in pieces:
        heights = jax.random.uniform(jax.random.fold_in(jax.random.fold_in(key, 6), position), (shards_of,), jnp.float32, low / len(pieces), top_value / len(pieces))
        gain = gain * jnp.repeat(jnp.exp(heights), shape[position] // shards_of).reshape((-1,) + (1,) * (len(shape) - 1 - position))
    return gain


def noise(stream_key, shape, spread, limit, cuts=(), held_as=jnp.bfloat16):
    array = spread * jax.random.normal(stream_key, shape, jnp.float32)
    if cuts:
        array = array * block_levels(stream_key, shape, cuts, -0.22, 0.18)
    return jnp.clip(array, -limit, limit).astype(held_as)


def setup_inputs(seed: int = 0) -> dict:
    key_of = jax.random.split(jax.random.key(seed), 14)
    node_latent = noise(key_of[0], (NODES, D), 1.0, 6.0, ((0, 128),))
    edge_latent = noise(key_of[1], (EDGES, D), 1.0, 6.0, ((0, 128),))
    edge_sender = set_ends(jax.random.randint(key_of[2], (EDGES,), 0, NODE_DEV + 4 * HALO), jax.random.fold_in(key_of[2], 1), 0, (NODE_DEV + 4 * HALO) - 1).astype(jnp.int32)
    edge_receiver = draw_edge_receiver(jax.random.fold_in(key_of[13], 71), 0)
    edge_count = draw_edge_count(jax.random.fold_in(key_of[13], 71), 0)
    halo_send = set_ends(jax.random.randint(key_of[5], (N_LON * N_LAT, 4, HALO), 0, NODE_DEV), jax.random.fold_in(key_of[5], 1), 0, NODE_DEV - 1).astype(jnp.int32)
    weight_in = noise(key_of[6], (3 * D, D), (3 * D) ** -0.5, 0.15625)
    bias_in = noise(key_of[7], (D,), 0.5, 3.0, (), jnp.float32)
    weight_out = noise(key_of[8], (D, D), D ** -0.5, 0.25)
    bias_out = noise(key_of[9], (D,), 0.5, 3.0, (), jnp.float32)
    norm_gain = jnp.clip(1.0 + 0.1 * jax.random.normal(key_of[10], (D,), jnp.float32), 0.5, 1.5)
    edge_cotangent = noise(key_of[11], (EDGES, D), 1.0, 6.0, ((0, 128),))
    node_cotangent = noise(key_of[12], (NODES, D), 1.0, 6.0, ((0, 128),))
    return {"node_latent": node_latent, "edge_latent": edge_latent, "edge_sender": edge_sender, "edge_receiver": edge_receiver, "edge_count": edge_count, "halo_send": halo_send, "weight_in": weight_in, "bias_in": bias_in, "weight_out": weight_out, "bias_out": bias_out, "norm_gain": norm_gain, "edge_cotangent": edge_cotangent, "node_cotangent": node_cotangent}


def edge_backward(ext, edge_lat, sender, receiver, count, edge_cot, node_cot, weight_in, bias_in, weight_out, bias_out, norm_gain):
    n_edges = edge_lat.shape[0]
    width = edge_lat.shape[1]
    live = (jnp.arange(n_edges, dtype=jnp.int32) < count).astype(jnp.float32)[:, None]
    joined = jnp.concatenate([edge_lat, jnp.take(ext, sender, axis=0), jnp.take(ext, receiver, axis=0)], axis=1)
    pre = jnp.dot(joined, weight_in, preferred_element_type=jnp.float32) + bias_in
    sig = jax.nn.sigmoid(pre)
    act = (pre * sig).astype(jnp.bfloat16)
    mixed = jnp.dot(act, weight_out, preferred_element_type=jnp.float32) + bias_out
    centred = mixed - lax.optimization_barrier(jnp.mean(mixed, axis=1, keepdims=True))
    scale = lax.rsqrt(lax.optimization_barrier(jnp.mean(centred * centred, axis=1, keepdims=True)) + 1e-05)
    normed = centred * scale
    upstream = live * (edge_cot.astype(jnp.float32) + jnp.take(node_cot, receiver, axis=0).astype(jnp.float32))
    grad_gain = lax.optimization_barrier(jnp.sum(upstream * normed, axis=0))
    scaled = upstream * norm_gain
    d_mixed = scale * (scaled - lax.optimization_barrier(jnp.mean(scaled, axis=1, keepdims=True)) - normed * lax.optimization_barrier(jnp.mean(scaled * normed, axis=1, keepdims=True)))
    d_mixed_b = d_mixed.astype(jnp.bfloat16)
    grad_b_out = lax.optimization_barrier(jnp.sum(d_mixed, axis=0))
    grad_w_out = lax.dot_general(act, d_mixed_b, (((0,), (0,)), ((), ())), preferred_element_type=jnp.float32)
    d_act = lax.dot_general(d_mixed_b, weight_out, (((1,), (1,)), ((), ())), preferred_element_type=jnp.float32)
    d_pre = d_act * sig * (1.0 + pre * (1.0 - sig))
    d_pre_b = d_pre.astype(jnp.bfloat16)
    grad_b_in = lax.optimization_barrier(jnp.sum(d_pre, axis=0))
    grad_w_in = lax.dot_general(joined, d_pre_b, (((0,), (0,)), ((), ())), preferred_element_type=jnp.float32)
    d_joined = lax.dot_general(d_pre_b, weight_in, (((1,), (1,)), ((), ())), preferred_element_type=jnp.float32)
    edge_grad = (live * (edge_cot.astype(jnp.float32) + d_joined[:, :width])).astype(jnp.bfloat16)
    table = jnp.zeros((ext.shape[0], width), jnp.float32)
    table = table.at[sender].add(d_joined[:, width:2 * width]).at[receiver].add(d_joined[:, 2 * width:])
    return (edge_grad, table, (grad_w_in, grad_b_in, grad_w_out, grad_b_out, grad_gain))

def reference(node_latent, edge_latent, edge_sender, edge_receiver, edge_count, halo_send, weight_in, bias_in, weight_out, bias_out, norm_gain, edge_cotangent, node_cotangent):
    n_lon = N_LON
    n_lat = N_LAT
    parts = n_lon * n_lat
    nodes = node_latent.reshape(n_lon, n_lat, NODE_DEV, D)
    lists = halo_send.reshape(n_lon, n_lat, 4 * HALO)
    rows = jnp.take_along_axis(nodes, lists[..., None], axis=2).reshape(n_lon, n_lat, 4, HALO, D)
    blank = jnp.zeros((n_lon, 1, HALO, D), jnp.bfloat16)
    slot_zero = jnp.roll(rows[:, :, 0], 1, axis=0)
    slot_one = jnp.roll(rows[:, :, 1], -1, axis=0)
    slot_two = jnp.concatenate([blank, rows[:, :-1, 2]], axis=1)
    slot_three = jnp.concatenate([rows[:, 1:, 3], blank], axis=1)
    ext = jnp.concatenate([nodes, slot_zero, slot_one, slot_two, slot_three], axis=2)
    ext = ext.reshape(parts, NODE_DEV + 4 * HALO, D)

    def step(carry, items):
        edge_grad, table, sums = edge_backward(*items, weight_in, bias_in, weight_out, bias_out, norm_gain)
        return (jax.tree.map(lambda a, b: a + b, carry, sums), (edge_grad, table))
    init = (jnp.zeros((3 * D, D), jnp.float32), jnp.zeros((D,), jnp.float32), jnp.zeros((D, D), jnp.float32), jnp.zeros((D,), jnp.float32), jnp.zeros((D,), jnp.float32))
    items = (ext, edge_latent.reshape(parts, EDGE_DEV, D), edge_sender.reshape(parts, EDGE_DEV), edge_receiver.reshape(parts, EDGE_DEV), edge_count, edge_cotangent.reshape(parts, EDGE_DEV, D), node_cotangent.reshape(parts, NODE_DEV, D))
    sums, (edge_grads, tables) = lax.scan(step, init, items)
    tables = tables.reshape(n_lon, n_lat, NODE_DEV + 4 * HALO, D)
    local = tables[:, :, :NODE_DEV]
    halo = lax.optimization_barrier(tables[:, :, NODE_DEV:].astype(jnp.bfloat16)).astype(jnp.float32)
    halo = halo.reshape(n_lon, n_lat, 4, HALO, D)
    zero_rows = jnp.zeros((n_lon, 1, HALO, D), jnp.float32)
    back_zero = jnp.roll(halo[:, :, 0], -1, axis=0)
    back_one = jnp.roll(halo[:, :, 1], 1, axis=0)
    back_two = jnp.concatenate([halo[:, 1:, 2], zero_rows], axis=1)
    back_three = jnp.concatenate([zero_rows, halo[:, :-1, 3]], axis=1)
    back = jnp.stack([back_zero, back_one, back_two, back_three], axis=2).reshape(n_lon, n_lat, 4 * HALO, D)
    adder = jax.vmap(jax.vmap(lambda base, index, extra: base.at[index].add(extra)))
    node_grad = adder(local, lists, back).reshape(NODES, D).astype(jnp.bfloat16)
    return (edge_grads.reshape(EDGES, D), node_grad, sums[0], sums[1], sums[2], sums[3], sums[4])
```

```python
import functools

import jax
import jax.numpy as jnp
from jax import lax
from jax.experimental import pallas as pl
from jax.experimental.pallas import tpu as pltpu
from jax.sharding import PartitionSpec as P

F32, BF16 = jnp.float32, jnp.bfloat16
MESH = pl.DeviceIdType.MESH
D = 512
NODE = 256
EDGE = 2048
HALO = 64
EXT = NODE + 4 * HALO
TABLE = EXT + NODE
HALF = D // 2
QUARTER = HALF // 4
SIXTEENTH = QUARTER // 4
BLOCK = 128
CHUNK = 256
OUT, EDGES_IN, SENDERS_IN, RECEIVERS_IN = range(4)
AXES = (("x", "y", "z"), ("y", "z", "x"), ("z", "x", "y"), ("x", "z", "y"))


def dot(a, b, contract=(1, 0)):
    dims = (((contract[0],), (contract[1],)), ((), ()))
    return lax.dot_general(a, b, dims, preferred_element_type=F32)


def where_am_i():
    lon, lat = lax.axis_index("lon"), lax.axis_index("lat")
    return lon, lat, lon % 2, (lon // 2) % 4, lon // 8


class Place:
    def __init__(self):
        self.lon, self.lat, self.core, self.y, self.z = where_am_i()
        self.at = {"x": self.lat, "y": self.y, "z": self.z}
        self.partner = (self.lon + 1 - 2 * self.core, self.lat)
        self.east = ((self.lon + 1) % 32, self.lat)
        self.west = ((self.lon + 31) % 32, self.lat)
        self.north = (self.lon, (self.lat + 1) % 4)
        self.south = (self.lon, (self.lat + 3) % 4)
        self.beyond = ((self.lon + 31 + 2 * self.core) % 32, self.lat)

    def other(self, axis, step):
        spot = (self.at[axis] + step) % 4
        if axis == "x":
            return spot, (self.lon, spot)
        if axis == "y":
            return spot, (self.z * 8 + spot * 2 + self.core, self.lat)
        return spot, (spot * 8 + self.y * 2 + self.core, self.lat)


def remote(src, dst, send, recv, device):
    return pltpu.make_async_remote_copy(
        src_ref=src, dst_ref=dst, send_sem=send, recv_sem=recv, device_id=device, device_id_type=MESH
    )


def rows_at(start, size, unit):
    return pl.ds(pl.multiple_of(start, unit), size)


def kernel(
    comm,
    node_hbm, edge_hbm, sender, receiver, count, lists, w_in_hbm, b_in, w_out_hbm, b_out, gain, cot_hbm, ncot_hbm,
    edge_grad_hbm, node_grad, summed, vectors,
    ext, edge, cot, w_in, w_out, ncot, load_sem, store_sem,
    rows, slots, back_out, back, halo_send, halo_recv,
    onehot, onehot_t, list_t, proj, pre0, act, slope, d_mix, d_pre, q, own_table,
    grads, half_out, half_in, s1, r1, h2, s2, r2, h3, s3, r3, m_send, m_recv,
    v_core, v_axes, v_send, v_recv,
):
    me = Place()
    n_chunks = EDGE // CHUNK

    node_in = pltpu.make_async_copy(node_hbm, ext.at[pl.ds(0, NODE)], load_sem.at[0])
    w_in_in = pltpu.make_async_copy(w_in_hbm, w_in, load_sem.at[1])
    edge_in = pltpu.make_async_copy(edge_hbm, edge, load_sem.at[2])
    ncot_in = pltpu.make_async_copy(ncot_hbm, ncot, load_sem.at[3])
    w_out_in = pltpu.make_async_copy(w_out_hbm, w_out, load_sem.at[4])
    cot_in = pltpu.make_async_copy(cot_hbm, cot, load_sem.at[5])
    for copy in (node_in, w_in_in, edge_in, ncot_in, w_out_in, cot_in):
        copy.start()

    if comm:
        barrier = pltpu.get_barrier_semaphore()
        peers = [me.partner, me.beyond] + [me.other(axis, k)[1] for axis in "xyz" for k in (1, 2, 3)]
        for peer in peers:
            pl.semaphore_signal(barrier, inc=1, device_id=peer, device_id_type=MESH)

    list_row = jnp.concatenate([lists[0, k : k + 1, :] for k in range(4)], axis=1)
    in_list = lax.broadcasted_iota(jnp.int32, (NODE, 4 * HALO), 0) == list_row
    list_t[...] = jnp.where(in_list, 1.0, 0.0).astype(BF16)
    node_in.wait()
    rows[...] = dot(list_t[...], ext[:NODE], (0, 0)).astype(BF16)
    halo_to = (me.east, me.west, me.north, me.south)
    halo_copies = [
        remote(rows.at[pl.ds(k * HALO, HALO)], slots.at[pl.ds(k * HALO, HALO)], halo_send.at[k], halo_recv.at[k], halo_to[k])
        for k in range(4)
    ]
    if comm:
        pl.semaphore_wait(barrier, len(peers))
        for copy in halo_copies:
            copy.start()
    else:
        slots[...] = rows[...]

    def tables(j, _):
        here = rows_at(j * BLOCK, BLOCK, BLOCK)
        for index, first, width in ((sender, 0, EXT), (receiver, EXT, NODE)):
            row = index[pl.ds(j, 1), :]
            wide = jnp.broadcast_to(row, (BLOCK, BLOCK))
            column = wide.T
            for k in range(width // BLOCK):
                lane = lax.broadcasted_iota(jnp.int32, (BLOCK, BLOCK), 1) + k * BLOCK
                line = lax.broadcasted_iota(jnp.int32, (BLOCK, BLOCK), 0) + k * BLOCK
                spot = pl.ds(first + k * BLOCK, BLOCK)
                onehot[here, spot] = jnp.where(column == lane, 1.0, 0.0).astype(BF16)
                onehot_t[spot, here] = jnp.where(line == wide, 1.0, 0.0).astype(BF16)
        return 0

    lax.fori_loop(0, EDGE // BLOCK, tables, 0)

    w_in_in.wait()
    proj[:NODE] = dot(ext[:NODE], w_in[D : 2 * D]).astype(BF16)
    proj[EXT:] = dot(ext[:NODE], w_in[2 * D :]).astype(BF16)

    edge_in.wait()

    def first_layer(c, _):
        here = rows_at(c * CHUNK, CHUNK, CHUNK)
        pre0[here] = dot(edge[here], w_in[:D]) + b_in[...]
        return 0

    lax.fori_loop(0, n_chunks, first_layer, 0)

    if comm:
        for copy in halo_copies:
            copy.wait_recv()
    inside = (None, None, (me.lat > 0).astype(BF16), (me.lat < 3).astype(BF16))
    for k in range(4):
        block = slots[k * HALO : (k + 1) * HALO]
        ext[NODE + k * HALO : NODE + (k + 1) * HALO] = block if inside[k] is None else block * inside[k]
    proj[NODE:EXT] = dot(ext[NODE:], w_in[D : 2 * D]).astype(BF16)

    ncot_in.wait()
    w_out_in.wait()
    cot_in.wait()

    def through(c, sums):
        sum_gain, sum_out, sum_in = sums
        here = rows_at(c * CHUNK, CHUNK, CHUNK)
        pre = pre0[here] + dot(onehot[here, :], proj[...])
        sig = 0.5 * jnp.tanh(0.5 * pre) + 0.5
        act_b = (pre * sig).astype(BF16)
        act[here] = act_b
        slope[...] = sig * (1.0 + pre * (1.0 - sig))
        mixed = dot(act_b, w_out[...]) + b_out[...]
        centred = mixed - jnp.mean(mixed, axis=1, keepdims=True)
        scale = lax.rsqrt(jnp.mean(centred * centred, axis=1, keepdims=True) + 1e-05)
        normed = centred * scale
        live = lax.broadcasted_iota(jnp.int32, (CHUNK, 1), 0) + c * CHUNK < count[0]
        at_node = dot(onehot[here, EXT:], ncot[...])
        upstream = jnp.where(live, cot[here].astype(F32) + at_node, 0.0)
        both = upstream * normed
        scaled = upstream * gain[...]
        mean_s = jnp.mean(scaled, axis=1, keepdims=True)
        mean_sn = jnp.mean(both * gain[...], axis=1, keepdims=True)
        d_mixed = scale * (scaled - mean_s - normed * mean_sn)
        d_mixed_b = d_mixed.astype(BF16)
        d_mix[here] = d_mixed_b
        d_p = dot(d_mixed_b, w_out[...], (1, 1)) * slope[...]
        d_pre[here] = d_p.astype(BF16)
        fold = lambda a: jnp.sum(a.reshape(CHUNK // 8, 8, D), axis=0)
        return sum_gain + fold(both), sum_out + fold(d_mixed), sum_in + fold(d_p)

    zero = jnp.zeros((8, D), F32)
    sum_gain, sum_out, sum_in = lax.fori_loop(0, n_chunks, through, (zero, zero, zero))

    line = lax.broadcasted_iota(jnp.int32, (8, D), 0)
    total = jnp.zeros((8, D), F32)
    for k, part in enumerate((sum_in, sum_out, sum_gain)):
        total = jnp.where(line == k, jnp.sum(part, axis=0, keepdims=True), total)
    started = []

    def start(copy):
        copy.start()
        started.append(copy)

    v_copies = {}

    def vector_send(stage):
        if stage == "core":
            copies = [remote(v_core.at[me.core], v_core.at[me.core], v_send.at[0], v_recv.at[0], me.partner)]
        else:
            n = "xyz".index(stage)
            spot = me.at[stage]
            copies = [
                remote(
                    v_axes.at[n, spot], v_axes.at[n, spot],
                    v_send.at[1 + 3 * n + k - 1], v_recv.at[1 + 3 * n + k - 1], me.other(stage, k)[1],
                )
                for k in (1, 2, 3)
            ]
        for copy in copies:
            start(copy)
        v_copies[stage] = copies

    def vector_sum(stage):
        for copy in v_copies[stage]:
            copy.wait_recv()
        if stage == "core":
            return v_core[0] + v_core[1]
        n = "xyz".index(stage)
        return (v_axes[n, 0] + v_axes[n, 1]) + (v_axes[n, 2] + v_axes[n, 3])

    if comm:
        v_core[me.core] = total
        vector_send("core")
    else:
        vectors[...] = total

    m_copies = {}

    def matrix_send(m, stage, copies):
        for copy in copies:
            start(copy)
        m_copies[m, stage] = copies

    def matrix_wait(m, stage):
        for copy in m_copies[m, stage]:
            copy.wait_recv()

    def sems(m, stage, k=1):
        n = 0 if stage == 0 else 1 + 3 * (stage - 1) + k - 1
        return m_send.at[m, n], m_recv.at[m, n]

    mine = me.core * HALF
    theirs = HALF - mine

    def gradient(m, compute):
        first = compute(pl.multiple_of(theirs, HALF))
        if comm:
            half_out[m] = first.astype(BF16)
            matrix_send(m, 0, [remote(half_out.at[m], half_in.at[m], *sems(m, 0), me.partner)])
        grads[m] = compute(pl.multiple_of(mine, HALF))
        if not comm:
            summed[m * D : m * D + HALF] = first.astype(BF16)
            summed[m * D + HALF : (m + 1) * D] = grads[m].astype(BF16)

    def stage_1(m):
        matrix_wait(m, 0)
        grads[m] = grads[m] + half_in[m].astype(F32)
        s1[m] = grads[m].astype(BF16)
        copies = []
        for k in (1, 2, 3):
            spot, device = me.other(AXES[m][0], k)
            copies.append(remote(s1.at[m, rows_at(spot * QUARTER, QUARTER, QUARTER)], r1.at[m, k - 1], *sems(m, 1, k), device))
        matrix_send(m, 1, copies)

    def stage_2(m):
        matrix_wait(m, 1)
        spot = me.at[AXES[m][0]]
        part = grads[m, rows_at(spot * QUARTER, QUARTER, QUARTER)]
        for k in range(3):
            part = part + r1[m, k].astype(F32)
        h2[m] = part
        s2[m] = part.astype(BF16)
        copies = []
        for k in (1, 2, 3):
            spot, device = me.other(AXES[m][1], k)
            copies.append(remote(s2.at[m, rows_at(spot * SIXTEENTH, SIXTEENTH, SIXTEENTH)], r2.at[m, k - 1], *sems(m, 2, k), device))
        matrix_send(m, 2, copies)

    def stage_3(m):
        matrix_wait(m, 2)
        spot = me.at[AXES[m][1]]
        part = h2[m, rows_at(spot * SIXTEENTH, SIXTEENTH, SIXTEENTH)]
        for k in range(3):
            part = part + r2[m, k].astype(F32)
        h3[m] = part
        s3[m] = part.astype(BF16)
        copies = []
        for k in (1, 2, 3):
            spot, device = me.other(AXES[m][2], k)
            copies.append(remote(s3.at[m, :, rows_at(spot * BLOCK, BLOCK, BLOCK)], r3.at[m, k - 1], *sems(m, 3, k), device))
        matrix_send(m, 3, copies)

    def line_of(m, depth):
        begin = m * D + mine
        if depth >= 1:
            begin = begin + me.at[AXES[m][0]] * QUARTER
        if depth >= 2:
            begin = begin + me.at[AXES[m][1]] * SIXTEENTH
        return rows_at(begin, (HALF, QUARTER, SIXTEENTH)[depth], SIXTEENTH)

    def stage_4(m):
        matrix_wait(m, 3)
        lane = rows_at(me.at[AXES[m][2]] * BLOCK, BLOCK, BLOCK)
        part = h3[m, :, lane]
        for k in range(3):
            part = part + r3[m, k].astype(F32)
        summed[line_of(m, 2), lane] = part.astype(BF16)
        block = summed.at[line_of(m, 2), lane]
        matrix_send(m, 4, [remote(block, block, *sems(m, 4, k), me.other(AXES[m][2], k)[1]) for k in (1, 2, 3)])

    def stage_5(m):
        matrix_wait(m, 4)
        block = summed.at[line_of(m, 2)]
        matrix_send(m, 5, [remote(block, block, *sems(m, 5, k), me.other(AXES[m][1], k)[1]) for k in (1, 2, 3)])

    def stage_6(m):
        matrix_wait(m, 5)
        block = summed.at[line_of(m, 1)]
        matrix_send(m, 6, [remote(block, block, *sems(m, 6, k), me.other(AXES[m][0], k)[1]) for k in (1, 2, 3)])

    def stage_7(m):
        matrix_wait(m, 6)
        block = summed.at[line_of(m, 0)]
        matrix_send(m, 7, [remote(block, block, *sems(m, 7), me.partner)])

    def stage_8(m):
        matrix_wait(m, 7)

    gradient(OUT, lambda at: dot(act[:, pl.ds(at, HALF)], d_mix[...], (0, 0)))
    gradient(EDGES_IN, lambda at: dot(edge[:, pl.ds(at, HALF)], d_pre[...], (0, 0)))
    if comm:
        stage_1(OUT)
    q[...] = dot(onehot_t[...], d_pre[...]).astype(BF16)
    if comm:
        stage_1(EDGES_IN)
    gradient(SENDERS_IN, lambda at: dot(ext[:, pl.ds(at, HALF)], q[:EXT], (0, 0)))
    gradient(RECEIVERS_IN, lambda at: dot(ext[:NODE, pl.ds(at, HALF)], q[EXT:], (0, 0)))
    back_out[...] = dot(q[NODE:EXT], w_in[D : 2 * D], (1, 1)).astype(BF16)
    back_to = (me.west, me.east, me.south, me.north)
    back_copies = [
        remote(back_out.at[pl.ds(k * HALO, HALO)], back.at[pl.ds(k * HALO, HALO)], halo_send.at[4 + k], halo_recv.at[4 + k], back_to[k])
        for k in range(4)
    ]
    if comm:
        for copy in back_copies:
            start(copy)
        stage_2(OUT)
        stage_1(SENDERS_IN)
        stage_1(RECEIVERS_IN)
        v_axes[0, me.lat] = vector_sum("core")
        vector_send("x")
        stage_2(EDGES_IN)
        stage_3(OUT)
    else:
        back[...] = back_out[...]

    own_table[...] = dot(q[:NODE], w_in[D : 2 * D], (1, 1)) + dot(q[EXT:], w_in[2 * D :], (1, 1))

    def last(c, _):
        here = rows_at(c * CHUNK, CHUNK, CHUNK)
        live = lax.broadcasted_iota(jnp.int32, (CHUNK, 1), 0) + c * CHUNK < count[0]
        d_edge = dot(d_pre[here], w_in[:D], (1, 1))
        act[here] = jnp.where(live, cot[here].astype(F32) + d_edge, 0.0).astype(BF16)
        return 0

    lax.fori_loop(0, n_chunks, last, 0)
    edge_grad_out = pltpu.make_async_copy(act, edge_grad_hbm, store_sem.at[0])
    edge_grad_out.start()

    if comm:
        stage_2(SENDERS_IN)
        stage_2(RECEIVERS_IN)
        stage_3(EDGES_IN)
        stage_4(OUT)
        v_axes[1, me.y] = vector_sum("x")
        vector_send("y")
        for copy in back_copies:
            copy.wait_recv()
    back_in = (None, None, (me.lat < 3).astype(BF16), (me.lat > 0).astype(BF16))
    for k in range(4):
        if back_in[k] is not None:
            back[k * HALO : (k + 1) * HALO] = back[k * HALO : (k + 1) * HALO] * back_in[k]
    node_grad[...] = (own_table[...] + dot(list_t[...], back[...])).astype(BF16)

    if comm:
        stage_3(SENDERS_IN)
        stage_3(RECEIVERS_IN)
        stage_4(EDGES_IN)
        stage_5(OUT)
        v_axes[2, me.z] = vector_sum("y")
        vector_send("z")
        stage_4(SENDERS_IN)
        stage_4(RECEIVERS_IN)
        stage_5(EDGES_IN)
        stage_6(OUT)
        vectors[...] = vector_sum("z")
        stage_5(SENDERS_IN)
        stage_5(RECEIVERS_IN)
        stage_6(EDGES_IN)
        stage_7(OUT)
        stage_6(SENDERS_IN)
        stage_6(RECEIVERS_IN)
        stage_7(EDGES_IN)
        stage_7(SENDERS_IN)
        stage_7(RECEIVERS_IN)
        for m in range(4):
            stage_8(m)
        for copy in halo_copies + started:
            copy.wait_send()
    edge_grad_out.wait()


def call(comm, *args):
    vmem = pl.BlockSpec(memory_space=pltpu.VMEM)
    hbm = pl.BlockSpec(memory_space=pl.ANY)
    smem = pl.BlockSpec(memory_space=pltpu.SMEM)
    V = pltpu.VMEM
    dma = pltpu.SemaphoreType.DMA
    return pl.pallas_call(
        functools.partial(kernel, comm),
        out_shape=(
            jax.ShapeDtypeStruct((EDGE, D), BF16),
            jax.ShapeDtypeStruct((NODE, D), BF16),
            jax.ShapeDtypeStruct((4 * D, D), BF16),
            jax.ShapeDtypeStruct((8, D), F32),
        ),
        in_specs=[hbm, hbm, vmem, vmem, smem, vmem, hbm, vmem, hbm, vmem, vmem, hbm, hbm],
        out_specs=(hbm, vmem, vmem, vmem),
        scratch_shapes=[
            V((EXT, D), BF16), V((EDGE, D), BF16), V((EDGE, D), BF16), V((3 * D, D), BF16), V((D, D), BF16),
            V((NODE, D), BF16), dma((6,)), dma((1,)),
            V((4 * HALO, D), BF16), V((4 * HALO, D), BF16), V((4 * HALO, D), BF16), V((4 * HALO, D), BF16),
            dma((8,)), dma((8,)),
            V((EDGE, TABLE), BF16), V((TABLE, EDGE), BF16), V((NODE, 4 * HALO), BF16), V((TABLE, D), BF16),
            V((EDGE, D), F32), V((EDGE, D), BF16), V((CHUNK, D), F32), V((EDGE, D), BF16), V((EDGE, D), BF16),
            V((TABLE, D), BF16), V((NODE, D), F32),
            V((4, HALF, D), F32), V((4, HALF, D), BF16), V((4, HALF, D), BF16), V((4, HALF, D), BF16),
            V((4, 3, QUARTER, D), BF16), V((4, QUARTER, D), F32), V((4, QUARTER, D), BF16),
            V((4, 3, SIXTEENTH, D), BF16), V((4, SIXTEENTH, D), F32), V((4, SIXTEENTH, D), BF16),
            V((4, 3, SIXTEENTH, BLOCK), BF16), dma((4, 22)), dma((4, 22)),
            V((2, 8, D), F32), V((3, 4, 8, D), F32), dma((10,)), dma((10,)),
        ],
        compiler_params=pltpu.CompilerParams(
            collective_id=0 if comm else None, has_side_effects=True, vmem_limit_bytes=56 * 2**20
        ),
    )(*args)


def body(
    node_latent, edge_latent, edge_sender, edge_receiver, edge_count, halo_send,
    weight_in, bias_in, weight_out, bias_out, norm_gain, edge_cotangent, node_cotangent, comm=True,
):
    edge_grad, node_grad, summed, vectors = call(
        comm,
        node_latent, edge_latent, edge_sender.reshape(EDGE // BLOCK, BLOCK), edge_receiver.reshape(EDGE // BLOCK, BLOCK),
        edge_count, halo_send, weight_in, bias_in.reshape(1, D), weight_out, bias_out.reshape(1, D),
        norm_gain.reshape(1, D), edge_cotangent, node_cotangent,
    )
    summed = summed.astype(F32)
    return edge_grad, node_grad, summed[D:], vectors[0], summed[:D], vectors[1], vectors[2]


def solution(mesh):
    both = P(("lon", "lat"))
    rows = P(("lon", "lat"), None)
    return jax.shard_map(
        body,
        mesh=mesh,
        in_specs=(rows, rows, both, both, both, P(("lon", "lat"), None, None), P(), P(), P(), P(), P(), rows, rows),
        out_specs=(rows, rows, P(), P(), P(), P(), P()),
        check_vma=False,
    )
```

```python
import functools

import jax
import jax.numpy as jnp
from jax import lax
from jax.experimental import pallas as pl
from jax.experimental.pallas import tpu as pltpu
from jax.sharding import PartitionSpec as P

F32, BF16 = jnp.float32, jnp.bfloat16
MESH = pl.DeviceIdType.MESH
D = 512
NODE = 256
EDGE = 2048
HALO = 64
EXT = NODE + 4 * HALO
TABLE = EXT + NODE
HALF = D // 2
QUARTER = HALF // 4
SIXTEENTH = QUARTER // 4
BLOCK = 128
CHUNK = 256
OUT, EDGES_IN, SENDERS_IN, RECEIVERS_IN = range(4)
AXES = (("x", "y", "z"), ("y", "z", "x"), ("z", "x", "y"), ("x", "z", "y"))
PLANE = [(i, j) for i in range(4) for j in range(4) if (i, j) != (0, 0)]
PLANE.sort(key=lambda step: -(min(step[0], 4 - step[0]) + min(step[1], 4 - step[1])))


def dot(a, b, contract=(1, 0)):
    dims = (((contract[0],), (contract[1],)), ((), ()))
    return lax.dot_general(a, b, dims, preferred_element_type=F32)


def where_am_i():
    lon, lat = lax.axis_index("lon"), lax.axis_index("lat")
    return lon, lat, lon % 2, (lon // 2) % 4, lon // 8


class Place:
    def __init__(self):
        self.lon, self.lat, self.core, self.y, self.z = where_am_i()
        self.at = {"x": self.lat, "y": self.y, "z": self.z}
        self.partner = (self.lon + 1 - 2 * self.core, self.lat)
        self.east = ((self.lon + 1) % 32, self.lat)
        self.west = ((self.lon + 31) % 32, self.lat)
        self.north = (self.lon, (self.lat + 1) % 4)
        self.south = (self.lon, (self.lat + 3) % 4)
        self.beyond = ((self.lon + 31 + 2 * self.core) % 32, self.lat)

    def other(self, axis, step):
        spot = (self.at[axis] + step) % 4
        return spot, self.device({axis: spot})

    def device(self, spots):
        at = {**self.at, **spots}
        return (at["z"] * 8 + at["y"] * 2 + self.core, at["x"])

    def plane(self, axes):
        found = []
        for step in PLANE:
            spots = [(self.at[axis] + by) % 4 for axis, by in zip(axes, step)]
            found.append((*spots, self.device(dict(zip(axes, spots)))))
        return found


def remote(src, dst, send, recv, device):
    return pltpu.make_async_remote_copy(
        src_ref=src, dst_ref=dst, send_sem=send, recv_sem=recv, device_id=device, device_id_type=MESH
    )


def rows_at(start, size, unit):
    return pl.ds(pl.multiple_of(start, unit), size)


def kernel(
    comm,
    node_hbm, edge_hbm, sender, receiver, count, lists, w_in_hbm, b_in, w_out_hbm, b_out, gain, cot_hbm, ncot_hbm,
    edge_grad, node_grad, sum_out, sum_in, vectors,
    ext, edge, cot, w_in, w_out, ncot, load_sem,
    rows, slots, back_out, back, halo_send, halo_recv,
    onehot, onehot_t, list_t, proj, pre0, act, slope, d_mix, d_pre, q, own_table,
    grads, half_out, half_in, s1, r1, h2, s2, r2, m_send, m_recv,
    v_core, v_axes, v_send, v_recv, plane_sem,
):
    me = Place()
    n_chunks = EDGE // CHUNK

    node_in = pltpu.make_async_copy(node_hbm, ext.at[pl.ds(0, NODE)], load_sem.at[0])
    w_in_in = pltpu.make_async_copy(w_in_hbm, w_in, load_sem.at[1])
    edge_in = pltpu.make_async_copy(edge_hbm, edge, load_sem.at[2])
    ncot_in = pltpu.make_async_copy(ncot_hbm, ncot, load_sem.at[3])
    w_out_in = pltpu.make_async_copy(w_out_hbm, w_out, load_sem.at[4])
    cot_in = pltpu.make_async_copy(cot_hbm, cot, load_sem.at[5])
    for copy in (node_in, w_in_in, edge_in, ncot_in, w_out_in, cot_in):
        copy.start()

    if comm:
        barrier = pltpu.get_barrier_semaphore()
        peers = [me.partner, me.beyond] + [me.other(axis, k)[1] for axis in "xyz" for k in (1, 2, 3)]
        for peer in peers:
            pl.semaphore_signal(barrier, inc=1, device_id=peer, device_id_type=MESH)

    list_row = jnp.concatenate([lists[0, k : k + 1, :] for k in range(4)], axis=1)
    in_list = lax.broadcasted_iota(jnp.int32, (NODE, 4 * HALO), 0) == list_row
    list_t[...] = jnp.where(in_list, 1.0, 0.0).astype(BF16)
    node_in.wait()
    rows[...] = dot(list_t[...], ext[:NODE], (0, 0)).astype(BF16)
    halo_to = (me.east, me.west, me.north, me.south)
    halo_copies = [
        remote(rows.at[pl.ds(k * HALO, HALO)], slots.at[pl.ds(k * HALO, HALO)], halo_send.at[k], halo_recv.at[k], halo_to[k])
        for k in range(4)
    ]
    if comm:
        pl.semaphore_wait(barrier, len(peers))
        for copy in halo_copies:
            copy.start()
        for peer in peers[2:]:
            pl.semaphore_signal(plane_sem, inc=1, device_id=peer, device_id_type=MESH)
    else:
        slots[...] = rows[...]

    def tables(j, _):
        here = rows_at(j * BLOCK, BLOCK, BLOCK)
        for index, first, width in ((sender, 0, EXT), (receiver, EXT, NODE)):
            row = index[pl.ds(j, 1), :]
            wide = jnp.broadcast_to(row, (BLOCK, BLOCK))
            column = wide.T
            for k in range(width // BLOCK):
                lane = lax.broadcasted_iota(jnp.int32, (BLOCK, BLOCK), 1) + k * BLOCK
                line = lax.broadcasted_iota(jnp.int32, (BLOCK, BLOCK), 0) + k * BLOCK
                spot = pl.ds(first + k * BLOCK, BLOCK)
                onehot[here, spot] = jnp.where(column == lane, 1.0, 0.0).astype(BF16)
                onehot_t[spot, here] = jnp.where(line == wide, 1.0, 0.0).astype(BF16)
        return 0

    lax.fori_loop(0, EDGE // BLOCK, tables, 0)

    w_in_in.wait()
    proj[:NODE] = dot(ext[:NODE], w_in[D : 2 * D]).astype(BF16)
    proj[EXT:] = dot(ext[:NODE], w_in[2 * D :]).astype(BF16)

    edge_in.wait()

    def first_layer(c, _):
        here = rows_at(c * CHUNK, CHUNK, CHUNK)
        pre0[here] = dot(edge[here], w_in[:D]) + b_in[...]
        return 0

    lax.fori_loop(0, n_chunks, first_layer, 0)

    if comm:
        for copy in halo_copies:
            copy.wait_recv()
    inside = (None, None, (me.lat > 0).astype(BF16), (me.lat < 3).astype(BF16))
    for k in range(4):
        block = slots[k * HALO : (k + 1) * HALO]
        ext[NODE + k * HALO : NODE + (k + 1) * HALO] = block if inside[k] is None else block * inside[k]
    proj[NODE:EXT] = dot(ext[NODE:], w_in[D : 2 * D]).astype(BF16)

    ncot_in.wait()
    w_out_in.wait()
    cot_in.wait()

    def through(c, sums):
        gain_rows, out_rows, in_rows = sums
        here = rows_at(c * CHUNK, CHUNK, CHUNK)
        pre = pre0[here] + dot(onehot[here, :], proj[...])
        sig = 0.5 * jnp.tanh(0.5 * pre) + 0.5
        act_b = (pre * sig).astype(BF16)
        act[here] = act_b
        slope[...] = sig * (1.0 + pre * (1.0 - sig))
        mixed = dot(act_b, w_out[...]) + b_out[...]
        centred = mixed - jnp.mean(mixed, axis=1, keepdims=True)
        scale = lax.rsqrt(jnp.mean(centred * centred, axis=1, keepdims=True) + 1e-05)
        normed = centred * scale
        live = lax.broadcasted_iota(jnp.int32, (CHUNK, 1), 0) + c * CHUNK < count[0]
        at_node = dot(onehot[here, EXT:], ncot[...])
        upstream = jnp.where(live, cot[here].astype(F32) + at_node, 0.0)
        both = upstream * normed
        scaled = upstream * gain[...]
        mean_s = jnp.mean(scaled, axis=1, keepdims=True)
        mean_sn = jnp.mean(both * gain[...], axis=1, keepdims=True)
        d_mixed = scale * (scaled - mean_s - normed * mean_sn)
        d_mixed_b = d_mixed.astype(BF16)
        d_mix[here] = d_mixed_b
        d_p = dot(d_mixed_b, w_out[...], (1, 1)) * slope[...]
        d_pre[here] = d_p.astype(BF16)
        fold = lambda a: jnp.sum(a.reshape(CHUNK // 8, 8, D), axis=0)
        return gain_rows + fold(both), out_rows + fold(d_mixed), in_rows + fold(d_p)

    zero = jnp.zeros((8, D), F32)
    gain_rows, out_rows, in_rows = lax.fori_loop(0, n_chunks, through, (zero, zero, zero))

    line = lax.broadcasted_iota(jnp.int32, (8, D), 0)
    total = jnp.zeros((8, D), F32)
    for k, part in enumerate((in_rows, out_rows, gain_rows)):
        total = jnp.where(line == k, jnp.sum(part, axis=0, keepdims=True), total)
    started = []

    def start(copy):
        copy.start()
        started.append(copy)

    v_copies = {}

    def vector_send(stage):
        if stage == "core":
            copies = [remote(v_core.at[me.core], v_core.at[me.core], v_send.at[0], v_recv.at[0], me.partner)]
        else:
            n = "xyz".index(stage)
            spot = me.at[stage]
            copies = [
                remote(
                    v_axes.at[n, spot], v_axes.at[n, spot],
                    v_send.at[1 + 3 * n + k - 1], v_recv.at[1 + 3 * n + k - 1], me.other(stage, k)[1],
                )
                for k in (1, 2, 3)
            ]
        for copy in copies:
            start(copy)
        v_copies[stage] = copies

    def vector_sum(stage):
        for copy in v_copies[stage]:
            copy.wait_recv()
        if stage == "core":
            return v_core[0] + v_core[1]
        n = "xyz".index(stage)
        return (v_axes[n, 0] + v_axes[n, 1]) + (v_axes[n, 2] + v_axes[n, 3])

    if comm:
        v_core[me.core] = total
        vector_send("core")
    else:
        vectors[...] = total

    m_copies = {}

    def matrix_send(m, stage, copies):
        for copy in copies:
            start(copy)
        m_copies[m, stage] = copies

    def matrix_wait(m, stage):
        for copy in m_copies[m, stage]:
            copy.wait_recv()

    def sems(m, stage, k=0):
        n = (0, 1, 4, 19, 34, 37)[stage] + k
        return m_send.at[m, n], m_recv.at[m, n]

    mine = me.core * HALF
    theirs = HALF - mine

    def gradient(m, compute):
        first = compute(pl.multiple_of(theirs, HALF))
        if comm:
            half_out[m] = first.astype(BF16)
            matrix_send(m, 0, [remote(half_out.at[m], half_in.at[m], *sems(m, 0), me.partner)])
        grads[m] = compute(pl.multiple_of(mine, HALF))
        if not comm:
            sum_out[:HALF] = first.astype(BF16)
            sum_out[HALF:] = grads[m].astype(BF16)
            sum_in[0] = sum_out[...]

    def stage_1(m):
        matrix_wait(m, 0)
        grads[m] = grads[m] + half_in[m].astype(F32)
        s1[m] = grads[m].astype(BF16)
        copies = []
        for k in range(3):
            spot, device = me.other(AXES[m][0], (2, 1, 3)[k])
            copies.append(remote(s1.at[m, rows_at(spot * QUARTER, QUARTER, QUARTER)], r1.at[m, k], *sems(m, 1, k), device))
        matrix_send(m, 1, copies)

    def stage_2(m):
        matrix_wait(m, 1)
        spot = me.at[AXES[m][0]]
        part = grads[m, rows_at(spot * QUARTER, QUARTER, QUARTER)]
        for k in range(3):
            part = part + r1[m, k].astype(F32)
        h2[m] = part
        s2[m] = part.astype(BF16)
        copies = []
        for k, (line, lane, device) in enumerate(me.plane(AXES[m][1:])):
            piece = s2.at[m, rows_at(line * SIXTEENTH, SIXTEENTH, SIXTEENTH), rows_at(lane * BLOCK, BLOCK, BLOCK)]
            copies.append(remote(piece, r2.at[m, k], *sems(m, 2, k), device))
        matrix_send(m, 2, copies)

    def block_of(m, depth):
        begin = mine
        if depth >= 1:
            begin = begin + me.at[AXES[m][0]] * QUARTER
        if depth >= 2:
            begin = begin + me.at[AXES[m][1]] * SIXTEENTH
        line = rows_at(begin, (HALF, QUARTER, SIXTEENTH)[depth], SIXTEENTH)
        if m == OUT:
            return sum_out.at[line]
        return sum_in.at[m - 1, line]

    def stage_3(m):
        matrix_wait(m, 2)
        lane = rows_at(me.at[AXES[m][2]] * BLOCK, BLOCK, BLOCK)
        part = h2[m, rows_at(me.at[AXES[m][1]] * SIXTEENTH, SIXTEENTH, SIXTEENTH), lane]
        for k in range(15):
            part = part + r2[m, k].astype(F32)
        block = block_of(m, 2).at[:, lane]
        block[...] = part.astype(BF16)
        peers = me.plane(AXES[m][1:])
        matrix_send(m, 3, [remote(block, block, *sems(m, 3, k), peers[k][2]) for k in range(15)])

    def stage_4(m):
        matrix_wait(m, 3)
        block = block_of(m, 1)
        matrix_send(m, 4, [remote(block, block, *sems(m, 4, k), me.other(AXES[m][0], (2, 1, 3)[k])[1]) for k in range(3)])

    def stage_5(m):
        matrix_wait(m, 4)
        block = block_of(m, 0)
        matrix_send(m, 5, [remote(block, block, *sems(m, 5), me.partner)])

    def stage_6(m):
        matrix_wait(m, 5)

    if comm:
        pl.semaphore_wait(plane_sem, 9)
    gradient(OUT, lambda at: dot(act[:, pl.ds(at, HALF)], d_mix[...], (0, 0)))
    q[...] = dot(onehot_t[...], d_pre[...]).astype(BF16)
    if comm:
        stage_1(OUT)
    gradient(SENDERS_IN, lambda at: dot(ext[:, pl.ds(at, HALF)], q[:EXT], (0, 0)))
    gradient(RECEIVERS_IN, lambda at: dot(ext[:NODE, pl.ds(at, HALF)], q[EXT:], (0, 0)))
    back_out[...] = dot(q[NODE:EXT], w_in[D : 2 * D], (1, 1)).astype(BF16)
    back_to = (me.west, me.east, me.south, me.north)
    back_copies = [
        remote(back_out.at[pl.ds(k * HALO, HALO)], back.at[pl.ds(k * HALO, HALO)], halo_send.at[4 + k], halo_recv.at[4 + k], back_to[k])
        for k in range(4)
    ]
    if comm:
        for copy in back_copies:
            start(copy)
        stage_1(SENDERS_IN)
        stage_1(RECEIVERS_IN)
    else:
        back[...] = back_out[...]
    gradient(EDGES_IN, lambda at: dot(edge[:, pl.ds(at, HALF)], d_pre[...], (0, 0)))
    if comm:
        stage_2(OUT)
        v_axes[0, me.lat] = vector_sum("core")
        vector_send("x")

    own_table[...] = dot(q[:NODE], w_in[D : 2 * D], (1, 1)) + dot(q[EXT:], w_in[2 * D :], (1, 1))
    if comm:
        stage_1(EDGES_IN)

    def last(c, _):
        here = rows_at(c * CHUNK, CHUNK, CHUNK)
        live = lax.broadcasted_iota(jnp.int32, (CHUNK, 1), 0) + c * CHUNK < count[0]
        d_edge = dot(d_pre[here], w_in[:D], (1, 1))
        edge_grad[here] = jnp.where(live, cot[here].astype(F32) + d_edge, 0.0).astype(BF16)
        return 0

    lax.fori_loop(0, n_chunks, last, 0)

    if comm:
        stage_2(SENDERS_IN)
        stage_2(RECEIVERS_IN)
        stage_2(EDGES_IN)
        stage_3(OUT)
        v_axes[1, me.y] = vector_sum("x")
        vector_send("y")
        for copy in back_copies:
            copy.wait_recv()
    back_in = (None, None, (me.lat < 3).astype(BF16), (me.lat > 0).astype(BF16))
    for k in range(4):
        if back_in[k] is not None:
            back[k * HALO : (k + 1) * HALO] = back[k * HALO : (k + 1) * HALO] * back_in[k]
    node_grad[...] = (own_table[...] + dot(list_t[...], back[...])).astype(BF16)

    if comm:
        stage_3(SENDERS_IN)
        stage_3(RECEIVERS_IN)
        stage_3(EDGES_IN)
        stage_4(OUT)
        v_axes[2, me.z] = vector_sum("y")
        vector_send("z")
        stage_4(SENDERS_IN)
        stage_4(RECEIVERS_IN)
        stage_4(EDGES_IN)
        stage_5(OUT)
        vectors[...] = vector_sum("z")
        stage_5(SENDERS_IN)
        stage_5(RECEIVERS_IN)
        stage_5(EDGES_IN)
        for m in range(4):
            stage_6(m)
        for copy in halo_copies + started:
            copy.wait_send()


def call(comm, *args):
    vmem = pl.BlockSpec(memory_space=pltpu.VMEM)
    hbm = pl.BlockSpec(memory_space=pltpu.HBM)
    smem = pl.BlockSpec(memory_space=pltpu.SMEM)
    V = pltpu.VMEM
    dma = pltpu.SemaphoreType.DMA
    return pl.pallas_call(
        functools.partial(kernel, comm),
        out_shape=(
            V((EDGE, D), BF16), V((NODE, D), BF16), V((D, D), BF16), V((3, D, D), BF16), V((8, D), F32),
        ),
        in_specs=[hbm, hbm, vmem, vmem, smem, vmem, hbm, vmem, hbm, vmem, vmem, hbm, hbm],
        out_specs=(vmem, vmem, vmem, vmem, vmem),
        scratch_shapes=[
            V((EXT, D), BF16), V((EDGE, D), BF16), V((EDGE, D), BF16), V((3 * D, D), BF16), V((D, D), BF16),
            V((NODE, D), BF16), dma((6,)),
            V((4 * HALO, D), BF16), V((4 * HALO, D), BF16), V((4 * HALO, D), BF16), V((4 * HALO, D), BF16),
            dma((8,)), dma((8,)),
            V((EDGE, TABLE), BF16), V((TABLE, EDGE), BF16), V((NODE, 4 * HALO), BF16), V((TABLE, D), BF16),
            V((EDGE, D), F32), V((EDGE, D), BF16), V((CHUNK, D), F32), V((EDGE, D), BF16), V((EDGE, D), BF16),
            V((TABLE, D), BF16), V((NODE, D), F32),
            V((4, HALF, D), F32), V((4, HALF, D), BF16), V((4, HALF, D), BF16), V((4, HALF, D), BF16),
            V((4, 3, QUARTER, D), BF16), V((4, QUARTER, D), F32), V((4, QUARTER, D), BF16),
            V((4, 15, SIXTEENTH, BLOCK), BF16), dma((4, 38)), dma((4, 38)),
            V((2, 8, D), F32), V((3, 4, 8, D), F32), dma((10,)), dma((10,)), pltpu.SemaphoreType.REGULAR,
        ],
        compiler_params=pltpu.CompilerParams(
            collective_id=0 if comm else None, has_side_effects=True, vmem_limit_bytes=57 * 2**20
        ),
    )(*args)


def finish_kernel(
    edge_grad, node_grad, sum_out, sum_in, vectors,
    edge_grad_hbm, node_grad_hbm, w_in_hbm, b_in_out, w_out_hbm, b_out_out, gain_out,
    wide, sem,
):
    copies = [
        pltpu.make_async_copy(edge_grad, edge_grad_hbm, sem.at[0]),
        pltpu.make_async_copy(node_grad, node_grad_hbm, sem.at[1]),
    ]
    for copy in copies:
        copy.start()
    for m in range(4):
        wide[m] = (sum_in[m] if m < 3 else sum_out[...]).astype(F32)
        to = w_in_hbm.at[pl.ds(m * D, D)] if m < 3 else w_out_hbm
        copies.append(pltpu.make_async_copy(wide.at[m], to, sem.at[2 + m]))
        copies[-1].start()
    for k, out in enumerate((b_in_out, b_out_out, gain_out)):
        out[...] = vectors[k : k + 1, :]
    for copy in copies:
        copy.wait()


def finish(*args):
    vmem = pl.BlockSpec(memory_space=pltpu.VMEM)
    hbm = pl.BlockSpec(memory_space=pltpu.HBM)
    vector = jax.ShapeDtypeStruct((1, D), F32)
    return pl.pallas_call(
        finish_kernel,
        out_shape=(
            jax.ShapeDtypeStruct((EDGE, D), BF16), jax.ShapeDtypeStruct((NODE, D), BF16),
            jax.ShapeDtypeStruct((3 * D, D), F32), vector, jax.ShapeDtypeStruct((D, D), F32), vector, vector,
        ),
        in_specs=[vmem] * 5,
        out_specs=(hbm, hbm, hbm, vmem, hbm, vmem, vmem),
        scratch_shapes=[pltpu.VMEM((4, D, D), F32), pltpu.SemaphoreType.DMA((6,))],
        compiler_params=pltpu.CompilerParams(vmem_limit_bytes=12 * 2**20),
    )(*args)


def body(
    node_latent, edge_latent, edge_sender, edge_receiver, edge_count, halo_send,
    weight_in, bias_in, weight_out, bias_out, norm_gain, edge_cotangent, node_cotangent, comm=True,
):
    results = call(
        comm,
        node_latent, edge_latent, edge_sender.reshape(EDGE // BLOCK, BLOCK), edge_receiver.reshape(EDGE // BLOCK, BLOCK),
        edge_count, halo_send, weight_in, bias_in.reshape(1, D), weight_out, bias_out.reshape(1, D),
        norm_gain.reshape(1, D), edge_cotangent, node_cotangent,
    )
    edge_grad, node_grad, w_in, b_in, w_out, b_out, gain = finish(*results)
    return edge_grad, node_grad, w_in, b_in.reshape(D), w_out, b_out.reshape(D), gain.reshape(D)


def solution(mesh):
    both = P(("lon", "lat"))
    rows = P(("lon", "lat"), None)
    return jax.shard_map(
        body,
        mesh=mesh,
        in_specs=(rows, rows, both, both, both, P(("lon", "lat"), None, None), P(), P(), P(), P(), P(), rows, rows),
        out_specs=(rows, rows, P(), P(), P(), P(), P()),
        check_vma=False,
    )
```

```python
import functools

import jax
import jax.numpy as jnp
from jax import lax
from jax.experimental import pallas as pl
from jax.experimental.pallas import tpu as pltpu
from jax.sharding import PartitionSpec as P

F32, BF16 = jnp.float32, jnp.bfloat16
MESH = pl.DeviceIdType.MESH
D = 512
NODE = 256
EDGE = 2048
HALO = 64
EXT = NODE + 4 * HALO
TABLE = EXT + NODE
HALF = D // 2
QUARTER = HALF // 4
SIXTEENTH = QUARTER // 4
BLOCK = 128
CHUNK = 1024
SUB = 32
UNROLL = True
OUT, EDGES_IN, SENDERS_IN, RECEIVERS_IN = range(4)
AXES = (("x", "y", "z"), ("y", "z", "x"), ("z", "x", "y"), ("x", "z", "y"))
PLANE = [(i, j) for i in range(4) for j in range(4) if (i, j) != (0, 0)]
PLANE.sort(key=lambda step: -(min(step[0], 4 - step[0]) + min(step[1], 4 - step[1])))


def dot(a, b, contract=(1, 0)):
    dims = (((contract[0],), (contract[1],)), ((), ()))
    return lax.dot_general(a, b, dims, preferred_element_type=F32)


def where_am_i():
    lon, lat = lax.axis_index("lon"), lax.axis_index("lat")
    return lon, lat, lon % 2, (lon // 2) % 4, lon // 8


class Place:
    def __init__(self):
        self.lon, self.lat, self.core, self.y, self.z = where_am_i()
        self.at = {"x": self.lat, "y": self.y, "z": self.z}
        self.partner = (self.lon + 1 - 2 * self.core, self.lat)
        self.east = ((self.lon + 1) % 32, self.lat)
        self.west = ((self.lon + 31) % 32, self.lat)
        self.north = (self.lon, (self.lat + 1) % 4)
        self.south = (self.lon, (self.lat + 3) % 4)
        self.beyond = ((self.lon + 31 + 2 * self.core) % 32, self.lat)

    def other(self, axis, step):
        spot = (self.at[axis] + step) % 4
        return spot, self.device({axis: spot})

    def device(self, spots):
        at = {**self.at, **spots}
        return (at["z"] * 8 + at["y"] * 2 + self.core, at["x"])

    def plane(self, axes):
        found = []
        for step in PLANE:
            spots = [(self.at[axis] + by) % 4 for axis, by in zip(axes, step)]
            found.append((*spots, self.device(dict(zip(axes, spots)))))
        return found


def remote(src, dst, send, recv, device):
    return pltpu.make_async_remote_copy(
        src_ref=src, dst_ref=dst, send_sem=send, recv_sem=recv, device_id=device, device_id_type=MESH
    )


def rows_at(start, size, unit):
    return pl.ds(pl.multiple_of(start, unit), size)


def kernel(
    comm,
    node_hbm, edge_hbm, sender_hbm, receiver_hbm, count, lists_hbm, w_in_hbm, b_in_hbm, w_out_hbm, b_out_hbm, gain_hbm, cot_hbm, ncot_hbm,
    edge_grad, node_grad, sum_out, sum_in, vectors,
    lists, sender, receiver, b_in, b_out, gain, ext, edge, cot, w_in, w_out, ncot, load_sem,
    rows, slots, back_out, back, halo_send, halo_recv,
    onehot, onehot_t, list_t, proj, pre0, act, slope, half, mixed_s, at_node, d_mix, d_pre, q, own_table,
    grads, half_out, half_in, s1, r1, h2, s2, r2, m_send, m_recv,
    v_core, v_axes, v_send, v_recv, plane_sem,
):
    me = Place()
    n_chunks = EDGE // CHUNK

    if comm:
        barrier = pltpu.get_barrier_semaphore()
        peers = [me.partner, me.beyond] + [me.other(axis, k)[1] for axis in "xyz" for k in (1, 3, 2)]
        for peer in peers:
            pl.semaphore_signal(barrier, inc=1, device_id=peer, device_id_type=MESH)

    loads = [
        pltpu.make_async_copy(src, dst, load_sem.at[n])
        for n, (src, dst) in enumerate((
            (lists_hbm, lists), (node_hbm, ext.at[pl.ds(0, NODE)]), (sender_hbm, sender), (receiver_hbm, receiver),
            (w_in_hbm, w_in), (b_in_hbm, b_in), (edge_hbm, edge), (w_out_hbm, w_out), (ncot_hbm, ncot),
            (b_out_hbm, b_out), (gain_hbm, gain), (cot_hbm, cot),
        ))
    ]
    for copy in loads:
        copy.start()

    loads[0].wait()
    list_row = jnp.concatenate([lists[0, k : k + 1, :] for k in range(4)], axis=1)
    in_list = lax.broadcasted_iota(jnp.int32, (NODE, 4 * HALO), 0) == list_row
    list_t[...] = jnp.where(in_list, 1.0, 0.0).astype(BF16)
    loads[1].wait()
    rows[...] = dot(list_t[...], ext[:NODE], (0, 0)).astype(BF16)
    halo_to = (me.east, me.west, me.north, me.south)
    halo_copies = [
        remote(rows.at[pl.ds(k * HALO, HALO)], slots.at[pl.ds(k * HALO, HALO)], halo_send.at[k], halo_recv.at[k], halo_to[k])
        for k in range(4)
    ]
    if comm:
        pl.semaphore_wait(barrier, len(peers))
        for copy in halo_copies:
            copy.start()
        for peer in peers[2:]:
            pl.semaphore_signal(plane_sem, inc=1, device_id=peer, device_id_type=MESH)
    else:
        slots[...] = rows[...]

    def tables(j, _):
        here = rows_at(j * BLOCK, BLOCK, BLOCK)
        for index, first, width in ((sender, 0, EXT), (receiver, EXT, NODE)):
            row = index[pl.ds(j, 1), :]
            wide = jnp.broadcast_to(row, (BLOCK, BLOCK))
            column = wide.T
            for k in range(width // BLOCK):
                lane = lax.broadcasted_iota(jnp.int32, (BLOCK, BLOCK), 1) + k * BLOCK
                line = lax.broadcasted_iota(jnp.int32, (BLOCK, BLOCK), 0) + k * BLOCK
                spot = pl.ds(first + k * BLOCK, BLOCK)
                onehot[here, spot] = jnp.where(column == lane, 1.0, 0.0).astype(BF16)
                onehot_t[spot, here] = jnp.where(line == wide, 1.0, 0.0).astype(BF16)
        return 0

    loads[2].wait()
    loads[3].wait()
    lax.fori_loop(0, EDGE // BLOCK, tables, 0)

    loads[4].wait()
    proj[:NODE] = (0.5 * dot(ext[:NODE], w_in[D : 2 * D])).astype(BF16)
    proj[EXT:] = (0.5 * dot(ext[:NODE], w_in[2 * D :])).astype(BF16)

    loads[5].wait()
    loads[6].wait()

    def first_layer(c, _):
        here = rows_at(c * CHUNK, CHUNK, CHUNK)
        pre0[here] = 0.5 * (dot(edge[here], w_in[:D]) + b_in[...])
        return 0

    lax.fori_loop(0, n_chunks, first_layer, 0)

    if comm:
        for copy in halo_copies:
            copy.wait_recv()
    inside = (None, None, (me.lat > 0).astype(BF16), (me.lat < 3).astype(BF16))
    for k in range(4):
        block = slots[k * HALO : (k + 1) * HALO]
        ext[NODE + k * HALO : NODE + (k + 1) * HALO] = block if inside[k] is None else block * inside[k]
    proj[NODE:EXT] = (0.5 * dot(ext[NODE:], w_in[D : 2 * D])).astype(BF16)

    for copy in loads[7:]:
        copy.wait()

    gain_row, b_out_row = gain[...], b_out[...]
    fold = lambda a: jnp.sum(a.reshape(-1, 8, D), axis=0)
    mean = lambda a: jnp.sum(a, axis=1, keepdims=True) * (1.0 / D)

    def through(c, sums):
        gain_rows, out_rows, in_rows = sums
        start = c * CHUNK
        here = rows_at(start, CHUNK, CHUNK)
        buf = c % 2 if isinstance(c, int) else 0
        half[buf] = pre0[here] + dot(onehot[here, :], proj[...])
        for r in range(0, CHUNK, SUB):
            there = rows_at(start + r, SUB, SUB)
            h = half[buf, r : r + SUB]
            u = 1.0 + jnp.tanh(h)
            a = h * u
            act[there] = a.astype(BF16)
            slope[buf, r : r + SUB] = a + (0.5 * u) * (1.0 - a)
        mixed_s[buf] = dot(act[here], w_out[...])
        at_node[buf] = dot(onehot[here, EXT:], ncot[...])
        for r in range(0, CHUNK, SUB):
            there = rows_at(start + r, SUB, SUB)
            mixed = mixed_s[buf, r : r + SUB] + b_out_row
            centred = mixed - mean(mixed)
            live = lax.broadcasted_iota(jnp.int32, (SUB, 1), 0) + (start + r) < count[0]
            scale = jnp.where(live, lax.rsqrt(mean(centred * centred) + 1e-05), 0.0)
            normed = centred * scale
            scaled = (cot[there].astype(F32) + at_node[buf, r : r + SUB]) * gain_row
            both = scaled * normed
            d_mixed = scaled * scale - mean(scaled) * scale - normed * (mean(both) * scale)
            d_mix[there] = d_mixed.astype(BF16)
            gain_rows, out_rows = gain_rows + fold(both), out_rows + fold(d_mixed)
        half[buf] = dot(d_mix[here], w_out[...], (1, 1))
        for r in range(0, CHUNK, SUB):
            there = rows_at(start + r, SUB, SUB)
            d_p = half[buf, r : r + SUB] * slope[buf, r : r + SUB]
            d_pre[there] = d_p.astype(BF16)
            in_rows = in_rows + fold(d_p)
        return gain_rows, out_rows, in_rows

    zero = jnp.zeros((8, D), F32)
    sums = (zero, zero, zero)
    if UNROLL:
        for c in range(n_chunks):
            sums = through(c, sums)
    else:
        sums = lax.fori_loop(0, n_chunks, through, sums)
    gain_rows, out_rows, in_rows = sums

    line = lax.broadcasted_iota(jnp.int32, (8, D), 0)
    total = jnp.zeros((8, D), F32)
    for k, part in enumerate((in_rows, out_rows, gain_rows)):
        part = jnp.sum(part, axis=0, keepdims=True)
        total = jnp.where(line == k, part / gain_row if k == 2 else part, total)
    started = []

    def start(copy):
        copy.start()
        started.append(copy)

    v_copies = {}

    def vector_send(stage):
        if stage == "core":
            copies = [remote(v_core.at[me.core], v_core.at[me.core], v_send.at[0], v_recv.at[0], me.partner)]
        else:
            n = "xyz".index(stage)
            spot = me.at[stage]
            copies = [
                remote(
                    v_axes.at[n, spot], v_axes.at[n, spot],
                    v_send.at[1 + 3 * n + k - 1], v_recv.at[1 + 3 * n + k - 1], me.other(stage, k)[1],
                )
                for k in (1, 2, 3)
            ]
        for copy in copies:
            start(copy)
        v_copies[stage] = copies

    def vector_sum(stage):
        for copy in v_copies[stage]:
            copy.wait_recv()
        if stage == "core":
            return v_core[0] + v_core[1]
        n = "xyz".index(stage)
        return (v_axes[n, 0] + v_axes[n, 1]) + (v_axes[n, 2] + v_axes[n, 3])

    if comm:
        v_core[me.core] = total
        vector_send("core")
    else:
        vectors[...] = total

    m_copies = {}

    def matrix_send(m, stage, copies):
        for copy in copies:
            start(copy)
        m_copies[m, stage] = copies

    def matrix_wait(m, stage):
        for copy in m_copies[m, stage]:
            copy.wait_recv()

    def sems(m, stage, k=0):
        n = (0, 1, 4, 19, 34, 37)[stage] + k
        return m_send.at[m, n], m_recv.at[m, n]

    mine = me.core * HALF
    theirs = HALF - mine

    def gradient(m, compute):
        first = compute(pl.multiple_of(theirs, HALF))
        if comm:
            half_out[m] = first.astype(BF16)
            matrix_send(m, 0, [remote(half_out.at[m], half_in.at[m], *sems(m, 0), me.partner)])
        grads[m] = compute(pl.multiple_of(mine, HALF))
        if not comm:
            sum_out[:HALF] = first.astype(BF16)
            sum_out[HALF:] = grads[m].astype(BF16)
            sum_in[0] = sum_out[...]

    def stage_1(m):
        matrix_wait(m, 0)
        grads[m] = grads[m] + half_in[m].astype(F32)
        s1[m] = grads[m].astype(BF16)
        copies = []
        for k in range(3):
            spot, device = me.other(AXES[m][0], (2, 1, 3)[k])
            copies.append(remote(s1.at[m, rows_at(spot * QUARTER, QUARTER, QUARTER)], r1.at[m, k], *sems(m, 1, k), device))
        matrix_send(m, 1, copies)

    def stage_2(m):
        matrix_wait(m, 1)
        spot = me.at[AXES[m][0]]
        part = grads[m, rows_at(spot * QUARTER, QUARTER, QUARTER)]
        for k in range(3):
            part = part + r1[m, k].astype(F32)
        h2[m] = part
        s2[m] = part.astype(BF16)
        copies = []
        for k, (line, lane, device) in enumerate(me.plane(AXES[m][1:])):
            piece = s2.at[m, rows_at(line * SIXTEENTH, SIXTEENTH, SIXTEENTH), rows_at(lane * BLOCK, BLOCK, BLOCK)]
            copies.append(remote(piece, r2.at[m, k], *sems(m, 2, k), device))
        matrix_send(m, 2, copies)

    def block_of(m, depth):
        begin = mine
        if depth >= 1:
            begin = begin + me.at[AXES[m][0]] * QUARTER
        if depth >= 2:
            begin = begin + me.at[AXES[m][1]] * SIXTEENTH
        line = rows_at(begin, (HALF, QUARTER, SIXTEENTH)[depth], SIXTEENTH)
        if m == OUT:
            return sum_out.at[line]
        return sum_in.at[m - 1, line]

    def stage_3(m):
        matrix_wait(m, 2)
        lane = rows_at(me.at[AXES[m][2]] * BLOCK, BLOCK, BLOCK)
        part = h2[m, rows_at(me.at[AXES[m][1]] * SIXTEENTH, SIXTEENTH, SIXTEENTH), lane]
        for k in range(15):
            part = part + r2[m, k].astype(F32)
        block = block_of(m, 2).at[:, lane]
        block[...] = part.astype(BF16)
        peers = me.plane(AXES[m][1:])
        matrix_send(m, 3, [remote(block, block, *sems(m, 3, k), peers[k][2]) for k in range(15)])

    def stage_4(m):
        matrix_wait(m, 3)
        block = block_of(m, 1)
        matrix_send(m, 4, [remote(block, block, *sems(m, 4, k), me.other(AXES[m][0], (2, 1, 3)[k])[1]) for k in range(3)])

    def stage_5(m):
        matrix_wait(m, 4)
        block = block_of(m, 0)
        matrix_send(m, 5, [remote(block, block, *sems(m, 5), me.partner)])

    def stage_6(m):
        matrix_wait(m, 5)

    if comm:
        pl.semaphore_wait(plane_sem, 9)
    gradient(OUT, lambda at: dot(act[:, pl.ds(at, HALF)], d_mix[...], (0, 0)))
    q[...] = dot(onehot_t[...], d_pre[...]).astype(BF16)
    if comm:
        stage_1(OUT)
    gradient(SENDERS_IN, lambda at: dot(ext[:, pl.ds(at, HALF)], q[:EXT], (0, 0)))
    gradient(RECEIVERS_IN, lambda at: dot(ext[:NODE, pl.ds(at, HALF)], q[EXT:], (0, 0)))
    back_out[...] = dot(q[NODE:EXT], w_in[D : 2 * D], (1, 1)).astype(BF16)
    back_to = (me.west, me.east, me.south, me.north)
    back_copies = [
        remote(back_out.at[pl.ds(k * HALO, HALO)], back.at[pl.ds(k * HALO, HALO)], halo_send.at[4 + k], halo_recv.at[4 + k], back_to[k])
        for k in range(4)
    ]
    if comm:
        for copy in back_copies:
            start(copy)
        stage_1(SENDERS_IN)
        stage_1(RECEIVERS_IN)
    else:
        back[...] = back_out[...]
    gradient(EDGES_IN, lambda at: dot(edge[:, pl.ds(at, HALF)], d_pre[...], (0, 0)))
    if comm:
        stage_2(OUT)
        v_axes[0, me.lat] = vector_sum("core")
        vector_send("x")

    own_table[...] = dot(q[:NODE], w_in[D : 2 * D], (1, 1)) + dot(q[EXT:], w_in[2 * D :], (1, 1))
    if comm:
        stage_1(EDGES_IN)

    def last(c, _):
        here = rows_at(c * CHUNK, CHUNK, CHUNK)
        live = lax.broadcasted_iota(jnp.int32, (CHUNK, 1), 0) + c * CHUNK < count[0]
        d_edge = dot(d_pre[here], w_in[:D], (1, 1))
        edge_grad[here] = jnp.where(live, cot[here].astype(F32) + d_edge, 0.0).astype(BF16)
        return 0

    lax.fori_loop(0, n_chunks, last, 0)

    if comm:
        stage_2(SENDERS_IN)
        stage_2(RECEIVERS_IN)
        stage_2(EDGES_IN)
        stage_3(OUT)
        v_axes[1, me.y] = vector_sum("x")
        vector_send("y")
        for copy in back_copies:
            copy.wait_recv()
    back_in = (None, None, (me.lat < 3).astype(BF16), (me.lat > 0).astype(BF16))
    for k in range(4):
        if back_in[k] is not None:
            back[k * HALO : (k + 1) * HALO] = back[k * HALO : (k + 1) * HALO] * back_in[k]
    node_grad[...] = (own_table[...] + dot(list_t[...], back[...])).astype(BF16)

    if comm:
        stage_3(SENDERS_IN)
        stage_3(RECEIVERS_IN)
        stage_3(EDGES_IN)
        stage_4(OUT)
        v_axes[2, me.z] = vector_sum("y")
        vector_send("z")
        stage_4(SENDERS_IN)
        stage_4(RECEIVERS_IN)
        stage_4(EDGES_IN)
        stage_5(OUT)
        vectors[...] = vector_sum("z")
        stage_5(SENDERS_IN)
        stage_5(RECEIVERS_IN)
        stage_5(EDGES_IN)
        for m in range(4):
            stage_6(m)
        for copy in halo_copies + started:
            copy.wait_send()


def call(comm, *args):
    vmem = pl.BlockSpec(memory_space=pltpu.VMEM)
    hbm = pl.BlockSpec(memory_space=pltpu.HBM)
    smem = pl.BlockSpec(memory_space=pltpu.SMEM)
    V = pltpu.VMEM
    dma = pltpu.SemaphoreType.DMA
    return pl.pallas_call(
        functools.partial(kernel, comm),
        out_shape=(
            V((EDGE, D), BF16), V((NODE, D), BF16), V((D, D), BF16), V((3, D, D), BF16), V((8, D), F32),
        ),
        in_specs=[hbm] * 4 + [smem] + [hbm] * 8,
        out_specs=(vmem, vmem, vmem, vmem, vmem),
        scratch_shapes=[
            V((1, 4, HALO), jnp.int32), V((EDGE // BLOCK, BLOCK), jnp.int32), V((EDGE // BLOCK, BLOCK), jnp.int32),
            V((1, D), F32), V((1, D), F32), V((1, D), F32),
            V((EXT, D), BF16), V((EDGE, D), BF16), V((EDGE, D), BF16), V((3 * D, D), BF16), V((D, D), BF16),
            V((NODE, D), BF16), dma((12,)),
            V((4 * HALO, D), BF16), V((4 * HALO, D), BF16), V((4 * HALO, D), BF16), V((4 * HALO, D), BF16),
            dma((8,)), dma((8,)),
            V((EDGE, TABLE), BF16), V((TABLE, EDGE), BF16), V((NODE, 4 * HALO), BF16), V((TABLE, D), BF16),
            V((EDGE, D), F32), V((EDGE, D), BF16), V((2, CHUNK, D), F32), V((2, CHUNK, D), F32), V((2, CHUNK, D), F32), V((2, CHUNK, D), F32),
            V((EDGE, D), BF16), V((EDGE, D), BF16),
            V((TABLE, D), BF16), V((NODE, D), F32),
            V((4, HALF, D), F32), V((4, HALF, D), BF16), V((4, HALF, D), BF16), V((4, HALF, D), BF16),
            V((4, 3, QUARTER, D), BF16), V((4, QUARTER, D), F32), V((4, QUARTER, D), BF16),
            V((4, 15, SIXTEENTH, BLOCK), BF16), dma((4, 38)), dma((4, 38)),
            V((2, 8, D), F32), V((3, 4, 8, D), F32), dma((10,)), dma((10,)), pltpu.SemaphoreType.REGULAR,
        ],
        compiler_params=pltpu.CompilerParams(
            collective_id=0 if comm else None, has_side_effects=True, vmem_limit_bytes=57 * 2**20
        ),
    )(*args)


def finish_kernel(
    edge_grad, node_grad, sum_out, sum_in, vectors,
    edge_grad_hbm, node_grad_hbm, w_in_hbm, b_in_out, w_out_hbm, b_out_out, gain_out,
    wide, sem,
):
    copies = [
        pltpu.make_async_copy(edge_grad, edge_grad_hbm, sem.at[0]),
        pltpu.make_async_copy(node_grad, node_grad_hbm, sem.at[1]),
    ]
    for copy in copies:
        copy.start()
    for m in range(4):
        wide[m] = (sum_in[m] if m < 3 else sum_out[...]).astype(F32)
        to = w_in_hbm.at[pl.ds(m * D, D)] if m < 3 else w_out_hbm
        copies.append(pltpu.make_async_copy(wide.at[m], to, sem.at[2 + m]))
        copies[-1].start()
    for k, out in enumerate((b_in_out, b_out_out, gain_out)):
        out[...] = vectors[k : k + 1, :]
    for copy in copies:
        copy.wait()


def finish(*args):
    vmem = pl.BlockSpec(memory_space=pltpu.VMEM)
    hbm = pl.BlockSpec(memory_space=pltpu.HBM)
    vector = jax.ShapeDtypeStruct((1, D), F32)
    return pl.pallas_call(
        finish_kernel,
        out_shape=(
            jax.ShapeDtypeStruct((EDGE, D), BF16), jax.ShapeDtypeStruct((NODE, D), BF16),
            jax.ShapeDtypeStruct((3 * D, D), F32), vector, jax.ShapeDtypeStruct((D, D), F32), vector, vector,
        ),
        in_specs=[vmem] * 5,
        out_specs=(hbm, hbm, hbm, vmem, hbm, vmem, vmem),
        scratch_shapes=[pltpu.VMEM((4, D, D), F32), pltpu.SemaphoreType.DMA((6,))],
        compiler_params=pltpu.CompilerParams(vmem_limit_bytes=12 * 2**20),
    )(*args)


def body(
    node_latent, edge_latent, edge_sender, edge_receiver, edge_count, halo_send,
    weight_in, bias_in, weight_out, bias_out, norm_gain, edge_cotangent, node_cotangent, comm=True,
):
    results = call(
        comm,
        node_latent, edge_latent, edge_sender.reshape(EDGE // BLOCK, BLOCK), edge_receiver.reshape(EDGE // BLOCK, BLOCK),
        edge_count, halo_send, weight_in, bias_in.reshape(1, D), weight_out, bias_out.reshape(1, D),
        norm_gain.reshape(1, D), edge_cotangent, node_cotangent,
    )
    edge_grad, node_grad, w_in, b_in, w_out, b_out, gain = finish(*results)
    return edge_grad, node_grad, w_in, b_in.reshape(D), w_out, b_out.reshape(D), gain.reshape(D)


def solution(mesh):
    both = P(("lon", "lat"))
    rows = P(("lon", "lat"), None)
    return jax.shard_map(
        body,
        mesh=mesh,
        in_specs=(rows, rows, both, both, both, P(("lon", "lat"), None, None), P(), P(), P(), P(), P(), rows, rows),
        out_specs=(rows, rows, P(), P(), P(), P(), P()),
        check_vma=False,
    )
```

```python
import functools

import jax
import jax.numpy as jnp
from jax import lax
from jax.experimental import pallas as pl
from jax.experimental.pallas import tpu as pltpu
from jax.sharding import PartitionSpec as P

F32, BF16 = jnp.float32, jnp.bfloat16
MESH = pl.DeviceIdType.MESH
D = 512
NODE = 256
EDGE = 2048
HALO = 64
EXT = NODE + 4 * HALO
TABLE = EXT + NODE
HALF = D // 2
QUARTER = HALF // 4
SIXTEENTH = QUARTER // 4
BLOCK = 128
CHUNK = 1024
SUB = 32
UNROLL = True
OUT, SENDERS_IN, RECEIVERS_IN, EDGES_IN = range(4)
AXES = (("x", "y", "z"), ("y", "z", "x"), ("z", "x", "y"), ("x", "z", "y"))
PLANE = [(i, j) for i in range(4) for j in range(4) if (i, j) != (0, 0)]
PLANE.sort(key=lambda step: -(min(step[0], 4 - step[0]) + min(step[1], 4 - step[1])))


def dot(a, b, contract=(1, 0)):
    dims = (((contract[0],), (contract[1],)), ((), ()))
    return lax.dot_general(a, b, dims, preferred_element_type=F32)


def where_am_i():
    lon, lat = lax.axis_index("lon"), lax.axis_index("lat")
    return lon, lat, lon % 2, (lon // 2) % 4, lon // 8


class Place:
    def __init__(self):
        self.lon, self.lat, self.core, self.y, self.z = where_am_i()
        self.at = {"x": self.lat, "y": self.y, "z": self.z}
        self.partner = (self.lon + 1 - 2 * self.core, self.lat)
        self.east = ((self.lon + 1) % 32, self.lat)
        self.west = ((self.lon + 31) % 32, self.lat)
        self.north = (self.lon, (self.lat + 1) % 4)
        self.south = (self.lon, (self.lat + 3) % 4)
        self.beyond = ((self.lon + 31 + 2 * self.core) % 32, self.lat)

    def other(self, axis, step):
        spot = (self.at[axis] + step) % 4
        return spot, self.device({axis: spot})

    def device(self, spots):
        at = {**self.at, **spots}
        return (at["z"] * 8 + at["y"] * 2 + self.core, at["x"])

    def plane(self, axes):
        found = []
        for step in PLANE:
            spots = [(self.at[axis] + by) % 4 for axis, by in zip(axes, step)]
            found.append((*spots, self.device(dict(zip(axes, spots)))))
        return found


def remote(src, dst, send, recv, device):
    return pltpu.make_async_remote_copy(
        src_ref=src, dst_ref=dst, send_sem=send, recv_sem=recv, device_id=device, device_id_type=MESH
    )


def arrived(like, sem):
    pltpu.make_async_copy(like, like, sem).wait()


def rows_at(start, size, unit):
    return pl.ds(pl.multiple_of(start, unit), size)


def kernel(
    comm,
    node_hbm, edge_hbm, sender_hbm, receiver_hbm, count_hbm, lists_hbm, w_in_hbm, b_in_hbm, w_out_hbm, b_out_hbm, gain_hbm, cot_hbm, ncot_hbm,
    edge_grad, node_grad, sum_out, sum_in, vectors,
    count, lists, sender, receiver, b_in, b_out, gain, ext, edge, cot, w_in, w_out, ncot, load_sem,
    rows, slots, back_out, back, halo_send, halo_recv,
    onehot, onehot_t, list_t, proj, pre0, act, slope, half, mixed_s, at_node, d_mix, d_pre, q, own_table,
    grads, half_out, half_in, s1, r1, h2, s2, r2, m_send, m_recv,
    v_core, v_axes, v_send, v_recv, plane_sem,
):
    me = Place()
    n_chunks = EDGE // CHUNK

    if comm:
        barrier = pltpu.get_barrier_semaphore()
        peers = [me.partner, me.beyond] + [me.other(axis, k)[1] for axis in "xyz" for k in (1, 3, 2)]
        for peer in peers:
            pl.semaphore_signal(barrier, inc=1, device_id=peer, device_id_type=MESH)

    loads = [
        pltpu.make_async_copy(src, dst, load_sem.at[n])
        for n, (src, dst) in enumerate((
            (lists_hbm, lists), (node_hbm, ext.at[pl.ds(0, NODE)]), (sender_hbm, sender), (receiver_hbm, receiver),
            (w_in_hbm, w_in), (b_in_hbm, b_in), (edge_hbm, edge), (w_out_hbm, w_out), (ncot_hbm, ncot),
            (b_out_hbm, b_out), (gain_hbm, gain), (count_hbm, count), (cot_hbm, cot),
        ))
    ]
    for copy in loads:
        copy.start()

    loads[0].wait()
    list_row = jnp.concatenate([lists[0, k : k + 1, :] for k in range(4)], axis=1)
    in_list = lax.broadcasted_iota(jnp.int32, (NODE, 4 * HALO), 0) == list_row
    list_t[...] = jnp.where(in_list, 1.0, 0.0).astype(BF16)
    loads[1].wait()
    rows[...] = dot(list_t[...], ext[:NODE], (0, 0)).astype(BF16)
    halo_to = (me.east, me.west, me.north, me.south)
    halo_copies = [
        remote(rows.at[pl.ds(k * HALO, HALO)], slots.at[pl.ds(k * HALO, HALO)], halo_send.at[0], halo_recv.at[0], halo_to[k])
        for k in range(4)
    ]
    if comm:
        pl.semaphore_wait(barrier, len(peers))
        for copy in halo_copies:
            copy.start()
        for peer in peers[2:]:
            pl.semaphore_signal(plane_sem, inc=1, device_id=peer, device_id_type=MESH)
    else:
        slots[...] = rows[...]

    def tables(j, _):
        here = rows_at(j * BLOCK, BLOCK, BLOCK)
        for index, first, width in ((sender, 0, EXT), (receiver, EXT, NODE)):
            row = index[pl.ds(j, 1), :]
            wide = jnp.broadcast_to(row, (BLOCK, BLOCK))
            column = wide.T
            for k in range(width // BLOCK):
                lane = lax.broadcasted_iota(jnp.int32, (BLOCK, BLOCK), 1) + k * BLOCK
                line = lax.broadcasted_iota(jnp.int32, (BLOCK, BLOCK), 0) + k * BLOCK
                spot = pl.ds(first + k * BLOCK, BLOCK)
                onehot[here, spot] = jnp.where(column == lane, 1.0, 0.0).astype(BF16)
                onehot_t[spot, here] = jnp.where(line == wide, 1.0, 0.0).astype(BF16)
        return 0

    loads[2].wait()
    loads[3].wait()
    lax.fori_loop(0, EDGE // BLOCK, tables, 0)

    loads[4].wait()
    proj[:NODE] = (0.5 * dot(ext[:NODE], w_in[D : 2 * D])).astype(BF16)
    proj[EXT:] = (0.5 * dot(ext[:NODE], w_in[2 * D :])).astype(BF16)

    loads[5].wait()
    loads[6].wait()

    def first_layer(c, _):
        here = rows_at(c * CHUNK, CHUNK, CHUNK)
        pre0[here] = 0.5 * (dot(edge[here], w_in[:D]) + b_in[...])
        return 0

    lax.fori_loop(0, n_chunks, first_layer, 0)

    if comm:
        arrived(slots, halo_recv.at[0])
    inside = (None, None, (me.lat > 0).astype(BF16), (me.lat < 3).astype(BF16))
    for k in range(4):
        block = slots[k * HALO : (k + 1) * HALO]
        ext[NODE + k * HALO : NODE + (k + 1) * HALO] = block if inside[k] is None else block * inside[k]
    proj[NODE:EXT] = (0.5 * dot(ext[NODE:], w_in[D : 2 * D])).astype(BF16)

    for copy in loads[7:]:
        copy.wait()

    gain_row, b_out_row = gain[...], b_out[...]
    fold = lambda a: jnp.sum(a.reshape(-1, 8, D), axis=0)
    mean = lambda a: jnp.sum(a, axis=1, keepdims=True) * (1.0 / D)

    def through(c, sums):
        gain_rows, out_rows, in_rows = sums
        start = c * CHUNK
        here = rows_at(start, CHUNK, CHUNK)
        buf = c % 2 if isinstance(c, int) else 0
        half[buf] = pre0[here] + dot(onehot[here, :], proj[...])
        for r in range(0, CHUNK, SUB):
            there = rows_at(start + r, SUB, SUB)
            h = half[buf, r : r + SUB]
            u = 1.0 + jnp.tanh(h)
            a = h * u
            act[there] = a.astype(BF16)
            slope[buf, r : r + SUB] = a + (0.5 * u) * (1.0 - a)
        mixed_s[buf] = dot(act[here], w_out[...])
        at_node[buf] = dot(onehot[here, EXT:], ncot[...])
        for r in range(0, CHUNK, SUB):
            there = rows_at(start + r, SUB, SUB)
            mixed = mixed_s[buf, r : r + SUB] + b_out_row
            centred = mixed - mean(mixed)
            live = lax.broadcasted_iota(jnp.int32, (SUB, 1), 0) + (start + r) < count[0]
            scale = jnp.where(live, lax.rsqrt(mean(centred * centred) + 1e-05), 0.0)
            normed = centred * scale
            scaled = (cot[there].astype(F32) + at_node[buf, r : r + SUB]) * gain_row
            both = scaled * normed
            d_mixed = scaled * scale - mean(scaled) * scale - normed * (mean(both) * scale)
            d_mix[there] = d_mixed.astype(BF16)
            gain_rows, out_rows = gain_rows + fold(both), out_rows + fold(d_mixed)
        half[buf] = dot(d_mix[here], w_out[...], (1, 1))
        for r in range(0, CHUNK, SUB):
            there = rows_at(start + r, SUB, SUB)
            d_p = half[buf, r : r + SUB] * slope[buf, r : r + SUB]
            d_pre[there] = d_p.astype(BF16)
            in_rows = in_rows + fold(d_p)
        return gain_rows, out_rows, in_rows

    zero = jnp.zeros((8, D), F32)
    sums = (zero, zero, zero)
    if UNROLL:
        for c in range(n_chunks):
            sums = through(c, sums)
    else:
        sums = lax.fori_loop(0, n_chunks, through, sums)
    gain_rows, out_rows, in_rows = sums

    line = lax.broadcasted_iota(jnp.int32, (8, D), 0)
    total = jnp.zeros((8, D), F32)
    for k, part in enumerate((in_rows, out_rows, gain_rows)):
        part = jnp.sum(part, axis=0, keepdims=True)
        total = jnp.where(line == k, part / gain_row if k == 2 else part, total)
    def vector_send(stage):
        if stage == "core":
            remote(v_core.at[me.core], v_core.at[me.core], v_send.at[0], v_recv.at[0], me.partner).start()
        else:
            n = "xyz".index(stage)
            here = v_axes.at[n, me.at[stage]]
            for k in (2, 1, 3):
                remote(here, here, v_send.at[1 + n], v_recv.at[1 + n], me.other(stage, k)[1]).start()

    def vector_sum(stage):
        if stage == "core":
            arrived(v_core.at[0], v_recv.at[0])
            return v_core[0] + v_core[1]
        n = "xyz".index(stage)
        arrived(v_axes.at[n, pl.ds(0, 3)], v_recv.at[1 + n])
        return (v_axes[n, 0] + v_axes[n, 1]) + (v_axes[n, 2] + v_axes[n, 3])

    if comm:
        v_core[me.core] = total
        vector_send("core")
    else:
        vectors[...] = total

    def matrix_send(m, stage, copies):
        for copy in copies:
            copy.start()

    def matrix_wait(m, stage):
        arrived(like(m, stage), m_recv.at[m, stage])

    def sems(m, stage):
        return m_send.at[m, stage], m_recv.at[m, stage]

    def like(m, stage):
        return (half_in, r1, r2, r2, r1, half_in)[stage].at[m]

    mine = me.core * HALF
    theirs = HALF - mine

    def gradient(m, compute):
        first = compute(pl.multiple_of(theirs, HALF))
        if comm:
            half_out[m] = first.astype(BF16)
            matrix_send(m, 0, [remote(half_out.at[m], half_in.at[m], *sems(m, 0), me.partner)])
        grads[m] = compute(pl.multiple_of(mine, HALF))
        if not comm:
            sum_out[:HALF] = first.astype(BF16)
            sum_out[HALF:] = grads[m].astype(BF16)
            sum_in[0] = sum_out[...]

    def stage_1(m):
        matrix_wait(m, 0)
        grads[m] = grads[m] + half_in[m].astype(F32)
        s1[m] = grads[m].astype(BF16)
        copies = []
        for k in range(3):
            spot, device = me.other(AXES[m][0], (2, 1, 3)[k])
            copies.append(remote(s1.at[m, rows_at(spot * QUARTER, QUARTER, QUARTER)], r1.at[m, k], *sems(m, 1), device))
        matrix_send(m, 1, copies)

    def stage_2(m):
        matrix_wait(m, 1)
        spot = me.at[AXES[m][0]]
        part = grads[m, rows_at(spot * QUARTER, QUARTER, QUARTER)]
        for k in range(3):
            part = part + r1[m, k].astype(F32)
        h2[m] = part
        s2[m] = part.astype(BF16)
        copies = []
        for k, (line, lane, device) in enumerate(me.plane(AXES[m][1:])):
            piece = s2.at[m, rows_at(line * SIXTEENTH, SIXTEENTH, SIXTEENTH), rows_at(lane * BLOCK, BLOCK, BLOCK)]
            copies.append(remote(piece, r2.at[m, k], *sems(m, 2), device))
        matrix_send(m, 2, copies)

    def block_of(m, depth):
        begin = mine
        if depth >= 1:
            begin = begin + me.at[AXES[m][0]] * QUARTER
        if depth >= 2:
            begin = begin + me.at[AXES[m][1]] * SIXTEENTH
        line = rows_at(begin, (HALF, QUARTER, SIXTEENTH)[depth], SIXTEENTH)
        if m == OUT:
            return sum_out.at[line]
        return sum_in.at[m % 3, line]

    def stage_3(m):
        matrix_wait(m, 2)
        lane = rows_at(me.at[AXES[m][2]] * BLOCK, BLOCK, BLOCK)
        part = h2[m, rows_at(me.at[AXES[m][1]] * SIXTEENTH, SIXTEENTH, SIXTEENTH), lane]
        for k in range(15):
            part = part + r2[m, k].astype(F32)
        block = block_of(m, 2).at[:, lane]
        block[...] = part.astype(BF16)
        peers = me.plane(AXES[m][1:])
        matrix_send(m, 3, [remote(block, block, *sems(m, 3), peers[k][2]) for k in range(15)])

    def stage_4(m):
        matrix_wait(m, 3)
        block = block_of(m, 1)
        matrix_send(m, 4, [remote(block, block, *sems(m, 4), me.other(AXES[m][0], (2, 1, 3)[k])[1]) for k in range(3)])

    def stage_5(m):
        matrix_wait(m, 4)
        block = block_of(m, 0)
        matrix_send(m, 5, [remote(block, block, *sems(m, 5), me.partner)])

    def stage_6(m):
        matrix_wait(m, 5)

    gradient(OUT, lambda at: dot(act[:, pl.ds(at, HALF)], d_mix[...], (0, 0)))
    q[...] = dot(onehot_t[...], d_pre[...]).astype(BF16)
    gradient(SENDERS_IN, lambda at: dot(ext[:, pl.ds(at, HALF)], q[:EXT], (0, 0)))
    gradient(RECEIVERS_IN, lambda at: dot(ext[:NODE, pl.ds(at, HALF)], q[EXT:], (0, 0)))
    back_out[...] = dot(q[NODE:EXT], w_in[D : 2 * D], (1, 1)).astype(BF16)
    back_to = (me.west, me.east, me.south, me.north)
    back_copies = [
        remote(back_out.at[pl.ds(k * HALO, HALO)], back.at[pl.ds(k * HALO, HALO)], halo_send.at[1], halo_recv.at[1], back_to[k])
        for k in range(4)
    ]
    if comm:
        stage_1(OUT)
        for copy in back_copies:
            copy.start()
    else:
        back[...] = back_out[...]
    gradient(EDGES_IN, lambda at: dot(edge[:, pl.ds(at, HALF)], d_pre[...], (0, 0)))
    if comm:
        stage_1(SENDERS_IN)
        stage_1(RECEIVERS_IN)
        v_axes[0, me.lat] = vector_sum("core")
        vector_send("x")
    own_table[...] = dot(q[:NODE], w_in[D : 2 * D], (1, 1)) + dot(q[EXT:], w_in[2 * D :], (1, 1))
    if comm:
        stage_1(EDGES_IN)

    def last(c, _):
        here = rows_at(c * CHUNK, CHUNK, CHUNK)
        live = lax.broadcasted_iota(jnp.int32, (CHUNK, 1), 0) + c * CHUNK < count[0]
        d_edge = dot(d_pre[here], w_in[:D], (1, 1))
        edge_grad[here] = jnp.where(live, cot[here].astype(F32) + d_edge, 0.0).astype(BF16)
        return 0

    lax.fori_loop(0, n_chunks, last, 0)

    if comm:
        pl.semaphore_wait(plane_sem, 9)
        for m in range(4):
            stage_2(m)
        v_axes[1, me.y] = vector_sum("x")
        vector_send("y")
        arrived(back, halo_recv.at[1])
    back_in = (None, None, (me.lat < 3).astype(BF16), (me.lat > 0).astype(BF16))
    for k in range(4):
        if back_in[k] is not None:
            back[k * HALO : (k + 1) * HALO] = back[k * HALO : (k + 1) * HALO] * back_in[k]
    node_grad[...] = (own_table[...] + dot(list_t[...], back[...])).astype(BF16)

    if comm:
        for m in range(4):
            stage_3(m)
        v_axes[2, me.z] = vector_sum("y")
        vector_send("z")
        for m in range(4):
            stage_4(m)
        vectors[...] = vector_sum("z")
        for m in range(4):
            stage_5(m)
        for m in range(4):
            stage_6(m)
        arrived(rows, halo_send.at[0])
        arrived(back_out, halo_send.at[1])
        arrived(v_core.at[0], v_send.at[0])
        for n in range(3):
            arrived(v_axes.at[n, pl.ds(0, 3)], v_send.at[1 + n])
        for m in range(4):
            for stage in range(6):
                arrived(like(m, stage), m_send.at[m, stage])


def call(comm, *args):
    vmem = pl.BlockSpec(memory_space=pltpu.VMEM)
    hbm = pl.BlockSpec(memory_space=pltpu.HBM)
    V = pltpu.VMEM
    dma = pltpu.SemaphoreType.DMA
    return pl.pallas_call(
        functools.partial(kernel, comm),
        out_shape=(
            V((EDGE, D), BF16), V((NODE, D), BF16), V((D, D), BF16), V((3, D, D), BF16), V((8, D), F32),
        ),
        in_specs=[hbm] * 13,
        out_specs=(vmem, vmem, vmem, vmem, vmem),
        scratch_shapes=[
            pltpu.SMEM((1,), jnp.int32), V((1, 4, HALO), jnp.int32), V((EDGE // BLOCK, BLOCK), jnp.int32), V((EDGE // BLOCK, BLOCK), jnp.int32),
            V((1, D), F32), V((1, D), F32), V((1, D), F32),
            V((EXT, D), BF16), V((EDGE, D), BF16), V((EDGE, D), BF16), V((3 * D, D), BF16), V((D, D), BF16),
            V((NODE, D), BF16), dma((13,)),
            V((4 * HALO, D), BF16), V((4 * HALO, D), BF16), V((4 * HALO, D), BF16), V((4 * HALO, D), BF16),
            dma((2,)), dma((2,)),
            V((EDGE, TABLE), BF16), V((TABLE, EDGE), BF16), V((NODE, 4 * HALO), BF16), V((TABLE, D), BF16),
            V((EDGE, D), F32), V((EDGE, D), BF16), V((2, CHUNK, D), F32), V((2, CHUNK, D), F32), V((2, CHUNK, D), F32), V((2, CHUNK, D), F32),
            V((EDGE, D), BF16), V((EDGE, D), BF16),
            V((TABLE, D), BF16), V((NODE, D), F32),
            V((4, HALF, D), F32), V((4, HALF, D), BF16), V((4, HALF, D), BF16), V((4, HALF, D), BF16),
            V((4, 3, QUARTER, D), BF16), V((4, QUARTER, D), F32), V((4, QUARTER, D), BF16),
            V((4, 15, SIXTEENTH, BLOCK), BF16), dma((4, 6)), dma((4, 6)),
            V((2, 8, D), F32), V((3, 4, 8, D), F32), dma((4,)), dma((4,)), pltpu.SemaphoreType.REGULAR,
        ],
        compiler_params=pltpu.CompilerParams(
            collective_id=0 if comm else None, has_side_effects=True, vmem_limit_bytes=57 * 2**20
        ),
    )(*args)


def finish_kernel(
    edge_grad, node_grad, sum_out, sum_in, vectors,
    edge_grad_hbm, node_grad_hbm, w_in_hbm, b_in_out, w_out_hbm, b_out_out, gain_out,
    wide, sem,
):
    copies = [
        pltpu.make_async_copy(edge_grad, edge_grad_hbm, sem.at[0]),
        pltpu.make_async_copy(node_grad, node_grad_hbm, sem.at[1]),
    ]
    for copy in copies:
        copy.start()
    for m in range(4):
        wide[m] = (sum_in[m] if m < 3 else sum_out[...]).astype(F32)
        to = w_in_hbm.at[pl.ds(m * D, D)] if m < 3 else w_out_hbm
        copies.append(pltpu.make_async_copy(wide.at[m], to, sem.at[2 + m]))
        copies[-1].start()
    for k, out in enumerate((b_in_out, b_out_out, gain_out)):
        out[...] = vectors[k : k + 1, :]
    for copy in copies:
        copy.wait()


def finish(*args):
    vmem = pl.BlockSpec(memory_space=pltpu.VMEM)
    hbm = pl.BlockSpec(memory_space=pltpu.HBM)
    vector = jax.ShapeDtypeStruct((1, D), F32)
    return pl.pallas_call(
        finish_kernel,
        out_shape=(
            jax.ShapeDtypeStruct((EDGE, D), BF16), jax.ShapeDtypeStruct((NODE, D), BF16),
            jax.ShapeDtypeStruct((3 * D, D), F32), vector, jax.ShapeDtypeStruct((D, D), F32), vector, vector,
        ),
        in_specs=[vmem] * 5,
        out_specs=(hbm, hbm, hbm, vmem, hbm, vmem, vmem),
        scratch_shapes=[pltpu.VMEM((4, D, D), F32), pltpu.SemaphoreType.DMA((6,))],
        compiler_params=pltpu.CompilerParams(vmem_limit_bytes=12 * 2**20),
    )(*args)


def body(
    node_latent, edge_latent, edge_sender, edge_receiver, edge_count, halo_send,
    weight_in, bias_in, weight_out, bias_out, norm_gain, edge_cotangent, node_cotangent, comm=True,
):
    results = call(
        comm,
        node_latent, edge_latent, edge_sender.reshape(EDGE // BLOCK, BLOCK), edge_receiver.reshape(EDGE // BLOCK, BLOCK),
        edge_count, halo_send, weight_in, bias_in.reshape(1, D), weight_out, bias_out.reshape(1, D),
        norm_gain.reshape(1, D), edge_cotangent, node_cotangent,
    )
    edge_grad, node_grad, w_in, b_in, w_out, b_out, gain = finish(*results)
    return edge_grad, node_grad, w_in, b_in.reshape(D), w_out, b_out.reshape(D), gain.reshape(D)


def solution(mesh):
    both = P(("lon", "lat"))
    rows = P(("lon", "lat"), None)
    return jax.shard_map(
        body,
        mesh=mesh,
        in_specs=(rows, rows, both, both, both, P(("lon", "lat"), None, None), P(), P(), P(), P(), P(), rows, rows),
        out_specs=(rows, rows, P(), P(), P(), P(), P()),
        check_vma=False,
    )
```

```python
import functools

import jax
import jax.numpy as jnp
from jax import lax
from jax.experimental import pallas as pl
from jax.experimental.pallas import tpu as pltpu
from jax.sharding import PartitionSpec as P

F32, BF16 = jnp.float32, jnp.bfloat16
MESH = pl.DeviceIdType.MESH
D = 512
NODE = 256
EDGE = 2048
HALO = 64
EXT = NODE + 4 * HALO
TABLE = EXT + NODE
HALF = D // 2
QUARTER = HALF // 4
SIXTEENTH = QUARTER // 4
BLOCK = 128
CHUNK = 1024
SUB = 32
OUT, SENDERS_IN, RECEIVERS_IN, EDGES_IN = range(4)
AXES = (("x", "y", "z"), ("y", "z", "x"), ("z", "x", "y"), ("x", "z", "y"))
PLANE = [(i, j) for i in range(4) for j in range(4) if (i, j) != (0, 0)]
PLANE.sort(key=lambda step: -(min(step[0], 4 - step[0]) + min(step[1], 4 - step[1])))


def dot(a, b, contract=(1, 0)):
    dims = (((contract[0],), (contract[1],)), ((), ()))
    return lax.dot_general(a, b, dims, preferred_element_type=F32)


def where_am_i():
    lon, lat = lax.axis_index("lon"), lax.axis_index("lat")
    return lon, lat, lon % 2, (lon // 2) % 4, lon // 8


class Place:
    def __init__(self):
        self.lon, self.lat, self.core, self.y, self.z = where_am_i()
        self.at = {"x": self.lat, "y": self.y, "z": self.z}
        self.partner = (self.lon + 1 - 2 * self.core, self.lat)
        self.east = ((self.lon + 1) % 32, self.lat)
        self.west = ((self.lon + 31) % 32, self.lat)
        self.north = (self.lon, (self.lat + 1) % 4)
        self.south = (self.lon, (self.lat + 3) % 4)
        self.beyond = ((self.lon + 31 + 2 * self.core) % 32, self.lat)

    def other(self, axis, step):
        spot = (self.at[axis] + step) % 4
        return spot, self.device({axis: spot})

    def device(self, spots):
        at = {**self.at, **spots}
        return (at["z"] * 8 + at["y"] * 2 + self.core, at["x"])

    def plane(self, axes):
        found = []
        for step in PLANE:
            spots = [(self.at[axis] + by) % 4 for axis, by in zip(axes, step)]
            found.append((*spots, self.device(dict(zip(axes, spots)))))
        return found


def remote(src, dst, send, recv, device):
    return pltpu.make_async_remote_copy(
        src_ref=src, dst_ref=dst, send_sem=send, recv_sem=recv, device_id=device, device_id_type=MESH
    )


def arrived(like, sem):
    pltpu.make_async_copy(like, like, sem).wait()


def rows_at(start, size, unit):
    return pl.ds(pl.multiple_of(start, unit), size)


def kernel(
    comm,
    node_hbm, edge_hbm, sender_hbm, receiver_hbm, count_hbm, lists_hbm, w_in_hbm, b_in_hbm, w_out_hbm, b_out_hbm, gain_hbm, cot_hbm, ncot_hbm,
    edge_grad, node_grad, sum_out, sum_in, vectors,
    count, lists, sender, receiver, b_in, b_out, gain, ext, edge, cot, w_in, w_out, ncot, load_sem,
    rows, slots, back_out, back, halo_send, halo_recv,
    onehot, onehot_t, list_t, proj, pre0, act, slope, half, mixed_s, at_node, acc_edge, acc_q, d_mix, d_pre, q, own_table,
    grads, half_out, half_in, s1, r1, h2, s2, r2, m_send, m_recv,
    v_core, v_axes, v_send, v_recv, plane_sem,
):
    me = Place()
    n_chunks = EDGE // CHUNK

    if comm:
        barrier = pltpu.get_barrier_semaphore()
        peers = [me.partner, me.beyond] + [me.other(axis, k)[1] for axis in "xyz" for k in (1, 3, 2)]
        for peer in peers:
            pl.semaphore_signal(barrier, inc=1, device_id=peer, device_id_type=MESH)

    loads = [
        pltpu.make_async_copy(src, dst, load_sem.at[n])
        for n, (src, dst) in enumerate((
            (lists_hbm, lists), (node_hbm, ext.at[pl.ds(0, NODE)]), (sender_hbm, sender), (receiver_hbm, receiver),
            (w_in_hbm, w_in), (b_in_hbm, b_in), (edge_hbm, edge), (w_out_hbm, w_out), (ncot_hbm, ncot),
            (b_out_hbm, b_out), (gain_hbm, gain), (count_hbm, count), (cot_hbm, cot),
        ))
    ]
    for copy in loads:
        copy.start()

    loads[0].wait()
    list_row = jnp.concatenate([lists[0, k : k + 1, :] for k in range(4)], axis=1)
    in_list = lax.broadcasted_iota(jnp.int32, (NODE, 4 * HALO), 0) == list_row
    list_t[...] = jnp.where(in_list, 1.0, 0.0).astype(BF16)
    loads[1].wait()
    rows[...] = dot(list_t[...], ext[:NODE], (0, 0)).astype(BF16)
    halo_to = (me.east, me.west, me.north, me.south)
    halo_copies = [
        remote(rows.at[pl.ds(k * HALO, HALO)], slots.at[pl.ds(k * HALO, HALO)], halo_send.at[0], halo_recv.at[0], halo_to[k])
        for k in range(4)
    ]
    if comm:
        pl.semaphore_wait(barrier, len(peers))
        for copy in halo_copies:
            copy.start()
        for peer in peers[2:]:
            pl.semaphore_signal(plane_sem, inc=1, device_id=peer, device_id_type=MESH)
    else:
        slots[...] = rows[...]

    def tables(j, _):
        here = rows_at(j * BLOCK, BLOCK, BLOCK)
        for index, first, width in ((sender, 0, EXT), (receiver, EXT, NODE)):
            row = index[pl.ds(j, 1), :]
            wide = jnp.broadcast_to(row, (BLOCK, BLOCK))
            column = wide.T
            for k in range(width // BLOCK):
                lane = lax.broadcasted_iota(jnp.int32, (BLOCK, BLOCK), 1) + k * BLOCK
                line = lax.broadcasted_iota(jnp.int32, (BLOCK, BLOCK), 0) + k * BLOCK
                spot = pl.ds(first + k * BLOCK, BLOCK)
                onehot[here, spot] = jnp.where(column == lane, 1.0, 0.0).astype(BF16)
                onehot_t[spot, here] = jnp.where(line == wide, 1.0, 0.0).astype(BF16)
        return 0

    loads[2].wait()
    loads[3].wait()
    lax.fori_loop(0, EDGE // BLOCK, tables, 0)

    loads[4].wait()
    proj[:NODE] = (0.5 * dot(ext[:NODE], w_in[D : 2 * D])).astype(BF16)
    proj[EXT:] = (0.5 * dot(ext[:NODE], w_in[2 * D :])).astype(BF16)

    loads[5].wait()
    loads[6].wait()

    def first_layer(c, _):
        here = rows_at(c * CHUNK, CHUNK, CHUNK)
        pre0[here] = 0.5 * (dot(edge[here], w_in[:D]) + b_in[...])
        return 0

    lax.fori_loop(0, n_chunks, first_layer, 0)

    if comm:
        arrived(slots, halo_recv.at[0])
    inside = (None, None, (me.lat > 0).astype(BF16), (me.lat < 3).astype(BF16))
    for k in range(4):
        block = slots[k * HALO : (k + 1) * HALO]
        ext[NODE + k * HALO : NODE + (k + 1) * HALO] = block if inside[k] is None else block * inside[k]
    proj[NODE:EXT] = (0.5 * dot(ext[NODE:], w_in[D : 2 * D])).astype(BF16)

    for copy in loads[7:]:
        copy.wait()

    gain_row, b_out_row = gain[...], b_out[...]
    fold = lambda a: jnp.sum(a.reshape(-1, 8, D), axis=0)
    mean = lambda a: jnp.sum(a, axis=1, keepdims=True) * (1.0 / D)

    def forward(c, sums):
        gain_rows, out_rows = sums
        start, buf = c * CHUNK, c
        here = pl.ds(start, CHUNK)
        half[buf] = pre0[here] + dot(onehot[here, :], proj[...])
        for r in range(0, CHUNK, SUB):
            there = pl.ds(start + r, SUB)
            h = half[buf, r : r + SUB]
            u = 1.0 + jnp.tanh(h)
            a = h * u
            act[there] = a.astype(BF16)
            slope[buf, r : r + SUB] = a + (0.5 * u) * (1.0 - a)
        mixed_s[buf] = dot(act[here], w_out[...])
        at_node[buf] = dot(onehot[here, EXT:], ncot[...])
        for r in range(0, CHUNK, SUB):
            there = pl.ds(start + r, SUB)
            mixed = mixed_s[buf, r : r + SUB] + b_out_row
            centred = mixed - mean(mixed)
            live = lax.broadcasted_iota(jnp.int32, (SUB, 1), 0) + (start + r) < count[0]
            scale = jnp.where(live, lax.rsqrt(mean(centred * centred) + 1e-05), 0.0)
            normed = centred * scale
            scaled = (cot[there].astype(F32) + at_node[buf, r : r + SUB]) * gain_row
            both = scaled * normed
            d_mixed = scaled * scale - mean(scaled) * scale - normed * (mean(both) * scale)
            d_mix[there] = d_mixed.astype(BF16)
            gain_rows, out_rows = gain_rows + fold(both), out_rows + fold(d_mixed)
        return gain_rows, out_rows

    def backward(c, in_rows):
        start, buf = c * CHUNK, c
        here = pl.ds(start, CHUNK)
        half[buf] = dot(d_mix[here], w_out[...], (1, 1))
        if c:
            before = pl.ds(start - CHUNK, CHUNK)
            new_edge = dot(edge[before], d_pre[before], (0, 0))
            new_q = dot(onehot_t[:, before], d_pre[before])
            acc_edge[...] = new_edge if c == 1 else acc_edge[...] + new_edge
            acc_q[...] = new_q if c == 1 else acc_q[...] + new_q
        for r in range(0, CHUNK, SUB):
            there = pl.ds(start + r, SUB)
            d_p = half[buf, r : r + SUB] * slope[buf, r : r + SUB]
            d_pre[there] = d_p.astype(BF16)
            in_rows = in_rows + fold(d_p)
        return in_rows

    def vector_send(stage):
        if stage == "core":
            remote(v_core.at[me.core], v_core.at[me.core], v_send.at[0], v_recv.at[0], me.partner).start()
        else:
            n = "xyz".index(stage)
            here = v_axes.at[n, me.at[stage]]
            for k in (2, 1, 3):
                remote(here, here, v_send.at[1 + n], v_recv.at[1 + n], me.other(stage, k)[1]).start()

    def vector_sum(stage):
        if stage == "core":
            arrived(v_core.at[0], v_recv.at[0])
            return v_core[0] + v_core[1]
        n = "xyz".index(stage)
        arrived(v_axes.at[n, pl.ds(0, 3)], v_recv.at[1 + n])
        return (v_axes[n, 0] + v_axes[n, 1]) + (v_axes[n, 2] + v_axes[n, 3])

    def matrix_send(m, stage, copies):
        for copy in copies:
            copy.start()

    def matrix_wait(m, stage):
        arrived(like(m, stage), m_recv.at[m, stage])

    def sems(m, stage):
        return m_send.at[m, stage], m_recv.at[m, stage]

    def like(m, stage):
        return (half_in, r1, r2, r2, r1, half_in)[stage].at[m]

    mine = me.core * HALF
    theirs = HALF - mine

    def gradient(m, compute):
        first = compute(pl.multiple_of(theirs, HALF))
        if comm:
            half_out[m] = first.astype(BF16)
            matrix_send(m, 0, [remote(half_out.at[m], half_in.at[m], *sems(m, 0), me.partner)])
        grads[m] = compute(pl.multiple_of(mine, HALF))
        if not comm:
            sum_out[:HALF] = first.astype(BF16)
            sum_out[HALF:] = grads[m].astype(BF16)
            sum_in[0] = sum_out[...]

    def stage_1(m):
        matrix_wait(m, 0)
        grads[m] = grads[m] + half_in[m].astype(F32)
        s1[m] = grads[m].astype(BF16)
        copies = []
        for k in range(3):
            spot, device = me.other(AXES[m][0], (2, 1, 3)[k])
            copies.append(remote(s1.at[m, rows_at(spot * QUARTER, QUARTER, QUARTER)], r1.at[m, k], *sems(m, 1), device))
        matrix_send(m, 1, copies)

    def stage_2(m):
        matrix_wait(m, 1)
        spot = me.at[AXES[m][0]]
        part = grads[m, rows_at(spot * QUARTER, QUARTER, QUARTER)]
        for k in range(3):
            part = part + r1[m, k].astype(F32)
        h2[m] = part
        s2[m] = part.astype(BF16)
        copies = []
        for k, (line, lane, device) in enumerate(me.plane(AXES[m][1:])):
            piece = s2.at[m, rows_at(line * SIXTEENTH, SIXTEENTH, SIXTEENTH), rows_at(lane * BLOCK, BLOCK, BLOCK)]
            copies.append(remote(piece, r2.at[m, k], *sems(m, 2), device))
        matrix_send(m, 2, copies)

    def block_of(m, depth):
        begin = mine
        if depth >= 1:
            begin = begin + me.at[AXES[m][0]] * QUARTER
        if depth >= 2:
            begin = begin + me.at[AXES[m][1]] * SIXTEENTH
        line = rows_at(begin, (HALF, QUARTER, SIXTEENTH)[depth], SIXTEENTH)
        if m == OUT:
            return sum_out.at[line]
        return sum_in.at[m % 3, line]

    def stage_3(m):
        matrix_wait(m, 2)
        lane = rows_at(me.at[AXES[m][2]] * BLOCK, BLOCK, BLOCK)
        part = h2[m, rows_at(me.at[AXES[m][1]] * SIXTEENTH, SIXTEENTH, SIXTEENTH), lane]
        for k in range(15):
            part = part + r2[m, k].astype(F32)
        block = block_of(m, 2).at[:, lane]
        block[...] = part.astype(BF16)
        peers = me.plane(AXES[m][1:])
        matrix_send(m, 3, [remote(block, block, *sems(m, 3), peers[k][2]) for k in range(15)])

    def stage_4(m):
        matrix_wait(m, 3)
        block = block_of(m, 1)
        matrix_send(m, 4, [remote(block, block, *sems(m, 4), me.other(AXES[m][0], (2, 1, 3)[k])[1]) for k in range(3)])

    def stage_5(m):
        matrix_wait(m, 4)
        block = block_of(m, 0)
        matrix_send(m, 5, [remote(block, block, *sems(m, 5), me.partner)])

    def stage_6(m):
        matrix_wait(m, 5)

    zero = jnp.zeros((8, D), F32)
    sums = (zero, zero)
    for c in range(n_chunks):
        sums = forward(c, sums)
    gain_rows, out_rows = sums
    gradient(OUT, lambda at: dot(act[:, pl.ds(at, HALF)], d_mix[...], (0, 0)))
    in_rows = zero
    for c in range(n_chunks):
        in_rows = backward(c, in_rows)

    line = lax.broadcasted_iota(jnp.int32, (8, D), 0)
    total = jnp.zeros((8, D), F32)
    for k, part in enumerate((in_rows, out_rows, gain_rows)):
        part = jnp.sum(part, axis=0, keepdims=True)
        total = jnp.where(line == k, part / gain_row if k == 2 else part, total)
    if comm:
        v_core[me.core] = total
        vector_send("core")
    else:
        vectors[...] = total

    if comm:
        stage_1(OUT)
    final = pl.ds(EDGE - CHUNK, CHUNK)
    q[...] = (acc_q[...] + dot(onehot_t[:, final], d_pre[final])).astype(BF16)
    gradient(SENDERS_IN, lambda at: dot(ext[:, pl.ds(at, HALF)], q[:EXT], (0, 0)))
    gradient(RECEIVERS_IN, lambda at: dot(ext[:NODE, pl.ds(at, HALF)], q[EXT:], (0, 0)))
    back_out[...] = dot(q[NODE:EXT], w_in[D : 2 * D], (1, 1)).astype(BF16)
    back_to = (me.west, me.east, me.south, me.north)
    back_copies = [
        remote(back_out.at[pl.ds(k * HALO, HALO)], back.at[pl.ds(k * HALO, HALO)], halo_send.at[1], halo_recv.at[1], back_to[k])
        for k in range(4)
    ]
    if comm:
        for copy in back_copies:
            copy.start()
    else:
        back[...] = back_out[...]
    gradient(EDGES_IN, lambda at: acc_edge[pl.ds(at, HALF)] + dot(edge[final, pl.ds(at, HALF)], d_pre[final], (0, 0)))
    if comm:
        stage_1(SENDERS_IN)
        stage_1(RECEIVERS_IN)
        v_axes[0, me.lat] = vector_sum("core")
        vector_send("x")
    own_table[...] = dot(q[:NODE], w_in[D : 2 * D], (1, 1)) + dot(q[EXT:], w_in[2 * D :], (1, 1))
    if comm:
        stage_1(EDGES_IN)

    def last(c, _):
        here = rows_at(c * CHUNK, CHUNK, CHUNK)
        live = lax.broadcasted_iota(jnp.int32, (CHUNK, 1), 0) + c * CHUNK < count[0]
        d_edge = dot(d_pre[here], w_in[:D], (1, 1))
        edge_grad[here] = jnp.where(live, cot[here].astype(F32) + d_edge, 0.0).astype(BF16)
        return 0

    lax.fori_loop(0, n_chunks, last, 0)

    if comm:
        pl.semaphore_wait(plane_sem, 9)
        for m in range(4):
            stage_2(m)
        v_axes[1, me.y] = vector_sum("x")
        vector_send("y")
        arrived(back, halo_recv.at[1])
    back_in = (None, None, (me.lat < 3).astype(BF16), (me.lat > 0).astype(BF16))
    for k in range(4):
        if back_in[k] is not None:
            back[k * HALO : (k + 1) * HALO] = back[k * HALO : (k + 1) * HALO] * back_in[k]
    node_grad[...] = (own_table[...] + dot(list_t[...], back[...])).astype(BF16)

    if comm:
        for m in range(4):
            stage_3(m)
        v_axes[2, me.z] = vector_sum("y")
        vector_send("z")
        for m in range(4):
            stage_4(m)
        vectors[...] = vector_sum("z")
        for m in range(4):
            stage_5(m)
        for m in range(4):
            stage_6(m)
        arrived(rows, halo_send.at[0])
        arrived(back_out, halo_send.at[1])
        arrived(v_core.at[0], v_send.at[0])
        for n in range(3):
            arrived(v_axes.at[n, pl.ds(0, 3)], v_send.at[1 + n])
        for m in range(4):
            for stage in range(6):
                arrived(like(m, stage), m_send.at[m, stage])


def call(comm, *args):
    vmem = pl.BlockSpec(memory_space=pltpu.VMEM)
    hbm = pl.BlockSpec(memory_space=pltpu.HBM)
    V = pltpu.VMEM
    dma = pltpu.SemaphoreType.DMA
    return pl.pallas_call(
        functools.partial(kernel, comm),
        out_shape=(
            V((EDGE, D), BF16), V((NODE, D), BF16), V((D, D), BF16), V((3, D, D), BF16), V((8, D), F32),
        ),
        in_specs=[hbm] * 13,
        out_specs=(vmem, vmem, vmem, vmem, vmem),
        scratch_shapes=[
            pltpu.SMEM((1,), jnp.int32), V((1, 4, HALO), jnp.int32), V((EDGE // BLOCK, BLOCK), jnp.int32), V((EDGE // BLOCK, BLOCK), jnp.int32),
            V((1, D), F32), V((1, D), F32), V((1, D), F32),
            V((EXT, D), BF16), V((EDGE, D), BF16), V((EDGE, D), BF16), V((3 * D, D), BF16), V((D, D), BF16),
            V((NODE, D), BF16), dma((13,)),
            V((4 * HALO, D), BF16), V((4 * HALO, D), BF16), V((4 * HALO, D), BF16), V((4 * HALO, D), BF16),
            dma((2,)), dma((2,)),
            V((EDGE, TABLE), BF16), V((TABLE, EDGE), BF16), V((NODE, 4 * HALO), BF16), V((TABLE, D), BF16),
            V((EDGE, D), F32), V((EDGE, D), BF16), V((2, CHUNK, D), F32), V((2, CHUNK, D), F32), V((2, CHUNK, D), F32), V((2, CHUNK, D), F32),
            V((D, D), F32), V((TABLE, D), F32),
            V((EDGE, D), BF16), V((EDGE, D), BF16),
            V((TABLE, D), BF16), V((NODE, D), F32),
            V((4, HALF, D), F32), V((4, HALF, D), BF16), V((4, HALF, D), BF16), V((4, HALF, D), BF16),
            V((4, 3, QUARTER, D), BF16), V((4, QUARTER, D), F32), V((4, QUARTER, D), BF16),
            V((4, 15, SIXTEENTH, BLOCK), BF16), dma((4, 6)), dma((4, 6)),
            V((2, 8, D), F32), V((3, 4, 8, D), F32), dma((4,)), dma((4,)), pltpu.SemaphoreType.REGULAR,
        ],
        compiler_params=pltpu.CompilerParams(
            collective_id=0 if comm else None, has_side_effects=True, vmem_limit_bytes=57 * 2**20
        ),
    )(*args)


def finish_kernel(
    edge_grad, node_grad, sum_out, sum_in, vectors,
    edge_grad_hbm, node_grad_hbm, w_in_hbm, b_in_out, w_out_hbm, b_out_out, gain_out,
    wide, sem,
):
    copies = [
        pltpu.make_async_copy(edge_grad, edge_grad_hbm, sem.at[0]),
        pltpu.make_async_copy(node_grad, node_grad_hbm, sem.at[1]),
        pltpu.make_async_copy(vectors.at[pl.ds(0, 1)], b_in_out, sem.at[6]),
        pltpu.make_async_copy(vectors.at[pl.ds(1, 1)], b_out_out, sem.at[7]),
        pltpu.make_async_copy(vectors.at[pl.ds(2, 1)], gain_out, sem.at[8]),
    ]
    for copy in copies:
        copy.start()
    for m in range(4):
        wide[m] = (sum_in[m] if m < 3 else sum_out[...]).astype(F32)
        to = w_in_hbm.at[pl.ds(m * D, D)] if m < 3 else w_out_hbm
        copies.append(pltpu.make_async_copy(wide.at[m], to, sem.at[2 + m]))
        copies[-1].start()
    for copy in copies:
        copy.wait()


def finish(*args):
    vmem = pl.BlockSpec(memory_space=pltpu.VMEM)
    hbm = pl.BlockSpec(memory_space=pltpu.HBM)
    vector = jax.ShapeDtypeStruct((1, D), F32)
    return pl.pallas_call(
        finish_kernel,
        out_shape=(
            jax.ShapeDtypeStruct((EDGE, D), BF16), jax.ShapeDtypeStruct((NODE, D), BF16),
            jax.ShapeDtypeStruct((3 * D, D), F32), vector, jax.ShapeDtypeStruct((D, D), F32), vector, vector,
        ),
        in_specs=[vmem] * 5,
        out_specs=(hbm,) * 7,
        scratch_shapes=[pltpu.VMEM((4, D, D), F32), pltpu.SemaphoreType.DMA((9,))],
        compiler_params=pltpu.CompilerParams(vmem_limit_bytes=12 * 2**20),
    )(*args)


def body(
    node_latent, edge_latent, edge_sender, edge_receiver, edge_count, halo_send,
    weight_in, bias_in, weight_out, bias_out, norm_gain, edge_cotangent, node_cotangent, comm=True,
):
    results = call(
        comm,
        node_latent, edge_latent, edge_sender.reshape(EDGE // BLOCK, BLOCK), edge_receiver.reshape(EDGE // BLOCK, BLOCK),
        edge_count, halo_send, weight_in, bias_in.reshape(1, D), weight_out, bias_out.reshape(1, D),
        norm_gain.reshape(1, D), edge_cotangent, node_cotangent,
    )
    edge_grad, node_grad, w_in, b_in, w_out, b_out, gain = finish(*results)
    return edge_grad, node_grad, w_in, b_in.reshape(D), w_out, b_out.reshape(D), gain.reshape(D)


def solution(mesh):
    both = P(("lon", "lat"))
    rows = P(("lon", "lat"), None)
    return jax.shard_map(
        body,
        mesh=mesh,
        in_specs=(rows, rows, both, both, both, P(("lon", "lat"), None, None), P(), P(), P(), P(), P(), rows, rows),
        out_specs=(rows, rows, P(), P(), P(), P(), P()),
        check_vma=False,
    )
```

```python
import functools

import jax
import jax.numpy as jnp
from jax import lax
from jax.experimental import pallas as pl
from jax.experimental.pallas import tpu as pltpu
from jax.sharding import PartitionSpec as P

F32, BF16 = jnp.float32, jnp.bfloat16
MESH = pl.DeviceIdType.MESH
D = 512
NODE = 256
EDGE = 2048
HALO = 64
EXT = NODE + 4 * HALO
TABLE = EXT + NODE
HALF = D // 2
QUARTER = HALF // 4
SIXTEENTH = QUARTER // 4
BLOCK = 128
CHUNK = 1024
SUB = 32
OUT, SENDERS_IN, RECEIVERS_IN, EDGES_IN = range(4)
AXES = (("x", "y", "z"), ("y", "z", "x"), ("z", "x", "y"), ("x", "z", "y"))
PLANE = [(i, j) for i in range(4) for j in range(4) if (i, j) != (0, 0)]
PLANE.sort(key=lambda step: -(min(step[0], 4 - step[0]) + min(step[1], 4 - step[1])))


def dot(a, b, contract=(1, 0)):
    dims = (((contract[0],), (contract[1],)), ((), ()))
    return lax.dot_general(a, b, dims, preferred_element_type=F32)


def where_am_i():
    lon, lat = lax.axis_index("lon"), lax.axis_index("lat")
    return lon, lat, lon % 2, (lon // 2) % 4, lon // 8


class Place:
    def __init__(self):
        self.lon, self.lat, self.core, self.y, self.z = where_am_i()
        self.at = {"x": self.lat, "y": self.y, "z": self.z}
        self.partner = (self.lon + 1 - 2 * self.core, self.lat)
        self.east = ((self.lon + 1) % 32, self.lat)
        self.west = ((self.lon + 31) % 32, self.lat)
        self.north = (self.lon, (self.lat + 1) % 4)
        self.south = (self.lon, (self.lat + 3) % 4)
        self.beyond = ((self.lon + 31 + 2 * self.core) % 32, self.lat)

    def other(self, axis, step):
        spot = (self.at[axis] + step) % 4
        return spot, self.device({axis: spot})

    def device(self, spots):
        at = {**self.at, **spots}
        return (at["z"] * 8 + at["y"] * 2 + self.core, at["x"])

    def plane(self, axes):
        found = []
        for step in PLANE:
            spots = [(self.at[axis] + by) % 4 for axis, by in zip(axes, step)]
            found.append((*spots, self.device(dict(zip(axes, spots)))))
        return found


def remote(src, dst, send, recv, device):
    return pltpu.make_async_remote_copy(
        src_ref=src, dst_ref=dst, send_sem=send, recv_sem=recv, device_id=device, device_id_type=MESH
    )


def arrived(like, sem):
    pltpu.make_async_copy(like, like, sem).wait()


def rows_at(start, size, unit):
    return pl.ds(pl.multiple_of(start, unit), size)


def kernel(
    comm,
    node_hbm, edge_hbm, sender_hbm, receiver_hbm, count_hbm, lists_hbm, w_in_hbm, b_in_hbm, w_out_hbm, b_out_hbm, gain_hbm, cot_hbm, ncot_hbm,
    edge_grad, node_grad, sum_out, sum_in, vectors,
    count, lists, sender, receiver, b_in, b_out, gain, ext, edge, cot, w_in, w_out, ncot, load_sem,
    rows, slots, back_out, back, halo_send, halo_recv,
    onehot, onehot_t, list_t, proj, pre0, act, slope, half, mixed_s, at_node, acc_out, acc_q, d_mix, d_pre, q, own_table,
    grads, half_out, half_in, s1, r1, h2, s2, r2, m_send, m_recv,
    v_core, v_axes, v_send, v_recv, plane_sem,
):
    me = Place()
    n_chunks = EDGE // CHUNK

    if comm:
        barrier = pltpu.get_barrier_semaphore()
        peers = [me.partner, me.beyond] + [me.other(axis, k)[1] for axis in "xyz" for k in (1, 3, 2)]
        for peer in peers:
            pl.semaphore_signal(barrier, inc=1, device_id=peer, device_id_type=MESH)

    loads = [
        pltpu.make_async_copy(src, dst, load_sem.at[n])
        for n, (src, dst) in enumerate((
            (lists_hbm, lists), (node_hbm, ext.at[pl.ds(0, NODE)]), (sender_hbm, sender), (receiver_hbm, receiver),
            (w_in_hbm, w_in), (b_in_hbm, b_in), (edge_hbm, edge), (w_out_hbm, w_out), (ncot_hbm, ncot),
            (b_out_hbm, b_out), (gain_hbm, gain), (count_hbm, count), (cot_hbm, cot),
        ))
    ]
    for copy in loads:
        copy.start()

    loads[0].wait()
    list_row = jnp.concatenate([lists[0, k : k + 1, :] for k in range(4)], axis=1)
    in_list = lax.broadcasted_iota(jnp.int32, (NODE, 4 * HALO), 0) == list_row
    list_t[...] = jnp.where(in_list, 1.0, 0.0).astype(BF16)
    loads[1].wait()
    rows[...] = dot(list_t[...], ext[:NODE], (0, 0)).astype(BF16)
    halo_to = (me.east, me.west, me.north, me.south)
    halo_copies = [
        remote(rows.at[pl.ds(k * HALO, HALO)], slots.at[pl.ds(k * HALO, HALO)], halo_send.at[0], halo_recv.at[0], halo_to[k])
        for k in range(4)
    ]
    if comm:
        pl.semaphore_wait(barrier, len(peers))
        for copy in halo_copies:
            copy.start()
        for peer in peers[2:]:
            pl.semaphore_signal(plane_sem, inc=1, device_id=peer, device_id_type=MESH)
    else:
        slots[...] = rows[...]

    def tables(j, _):
        here = rows_at(j * BLOCK, BLOCK, BLOCK)
        for index, first, width in ((sender, 0, EXT), (receiver, EXT, NODE)):
            row = index[pl.ds(j, 1), :]
            wide = jnp.broadcast_to(row, (BLOCK, BLOCK))
            column = wide.T
            for k in range(width // BLOCK):
                lane = lax.broadcasted_iota(jnp.int32, (BLOCK, BLOCK), 1) + k * BLOCK
                line = lax.broadcasted_iota(jnp.int32, (BLOCK, BLOCK), 0) + k * BLOCK
                spot = pl.ds(first + k * BLOCK, BLOCK)
                onehot[here, spot] = jnp.where(column == lane, 1.0, 0.0).astype(BF16)
                onehot_t[spot, here] = jnp.where(line == wide, 1.0, 0.0).astype(BF16)
        return 0

    loads[2].wait()
    loads[3].wait()
    lax.fori_loop(0, EDGE // BLOCK, tables, 0)

    loads[4].wait()
    proj[:NODE] = (0.5 * dot(ext[:NODE], w_in[D : 2 * D])).astype(BF16)
    proj[EXT:] = (0.5 * dot(ext[:NODE], w_in[2 * D :])).astype(BF16)

    loads[5].wait()
    loads[6].wait()

    def first_layer(c, _):
        here = rows_at(c * CHUNK, CHUNK, CHUNK)
        pre0[here] = 0.5 * (dot(edge[here], w_in[:D]) + b_in[...])
        return 0

    lax.fori_loop(0, n_chunks, first_layer, 0)

    if comm:
        arrived(slots, halo_recv.at[0])
    inside = (None, None, (me.lat > 0).astype(BF16), (me.lat < 3).astype(BF16))
    for k in range(4):
        block = slots[k * HALO : (k + 1) * HALO]
        ext[NODE + k * HALO : NODE + (k + 1) * HALO] = block if inside[k] is None else block * inside[k]
    proj[NODE:EXT] = (0.5 * dot(ext[NODE:], w_in[D : 2 * D])).astype(BF16)

    for copy in loads[7:]:
        copy.wait()

    gain_row, b_out_row = gain[...], b_out[...]
    fold = lambda a: jnp.sum(a.reshape(-1, 8, D), axis=0)
    mean = lambda a: jnp.sum(a, axis=1, keepdims=True) * (1.0 / D)

    def forward(c, sums):
        gain_rows, out_rows = sums
        start, buf = c * CHUNK, c
        here = pl.ds(start, CHUNK)
        half[buf] = pre0[here] + dot(onehot[here, :], proj[...])
        for r in range(0, CHUNK, SUB):
            there = pl.ds(start + r, SUB)
            h = half[buf, r : r + SUB]
            u = 1.0 + jnp.tanh(h)
            a = h * u
            act[there] = a.astype(BF16)
            slope[buf, r : r + SUB] = a + (0.5 * u) * (1.0 - a)
        mixed_s[buf] = dot(act[here], w_out[...])
        at_node[buf] = dot(onehot[here, EXT:], ncot[...])
        if c:
            acc_out[...] = dot(act[:CHUNK], d_mix[:CHUNK], (0, 0))
        for r in range(0, CHUNK, SUB):
            there = pl.ds(start + r, SUB)
            mixed = mixed_s[buf, r : r + SUB] + b_out_row
            centred = mixed - mean(mixed)
            live = lax.broadcasted_iota(jnp.int32, (SUB, 1), 0) + (start + r) < count[0]
            scale = jnp.where(live, lax.rsqrt(mean(centred * centred) + 1e-05), 0.0)
            normed = centred * scale
            scaled = (cot[there].astype(F32) + at_node[buf, r : r + SUB]) * gain_row
            both = scaled * normed
            d_mixed = scaled * scale - mean(scaled) * scale - normed * (mean(both) * scale)
            d_mix[there] = d_mixed.astype(BF16)
            gain_rows, out_rows = gain_rows + fold(both), out_rows + fold(d_mixed)
        return gain_rows, out_rows

    def backward(c, in_rows):
        start, buf = c * CHUNK, c
        here = pl.ds(start, CHUNK)
        half[buf] = dot(d_mix[here], w_out[...], (1, 1))
        for r in range(0, CHUNK, SUB):
            there = pl.ds(start + r, SUB)
            d_p = half[buf, r : r + SUB] * slope[buf, r : r + SUB]
            d_pre[there] = d_p.astype(BF16)
            in_rows = in_rows + fold(d_p)
        return in_rows

    def vector_send(stage):
        if stage == "core":
            remote(v_core.at[me.core], v_core.at[me.core], v_send.at[0], v_recv.at[0], me.partner).start()
        else:
            n = "xyz".index(stage)
            here = v_axes.at[n, me.at[stage]]
            for k in (2, 1, 3):
                remote(here, here, v_send.at[1 + n], v_recv.at[1 + n], me.other(stage, k)[1]).start()

    def vector_sum(stage):
        if stage == "core":
            arrived(v_core.at[0], v_recv.at[0])
            return v_core[0] + v_core[1]
        n = "xyz".index(stage)
        arrived(v_axes.at[n, pl.ds(0, 3)], v_recv.at[1 + n])
        return (v_axes[n, 0] + v_axes[n, 1]) + (v_axes[n, 2] + v_axes[n, 3])

    def matrix_send(m, stage, copies):
        for copy in copies:
            copy.start()

    def matrix_wait(m, stage):
        arrived(like(m, stage), m_recv.at[m, stage])

    def sems(m, stage):
        return m_send.at[m, stage], m_recv.at[m, stage]

    def like(m, stage):
        return (half_in, r1, r2, r2, r1, half_in)[stage].at[m]

    mine = me.core * HALF
    theirs = HALF - mine

    def gradient_theirs(m, compute):
        part = compute(pl.multiple_of(theirs, HALF)).astype(BF16)
        if comm:
            half_out[m] = part
            matrix_send(m, 0, [remote(half_out.at[m], half_in.at[m], *sems(m, 0), me.partner)])
        else:
            sum_out[:HALF] = part

    def gradient_mine(m, compute):
        grads[m] = compute(pl.multiple_of(mine, HALF))
        if not comm:
            sum_out[HALF:] = grads[m].astype(BF16)
            sum_in[0] = sum_out[...]

    def stage_1(m):
        matrix_wait(m, 0)
        grads[m] = grads[m] + half_in[m].astype(F32)
        s1[m] = grads[m].astype(BF16)
        copies = []
        for k in range(3):
            spot, device = me.other(AXES[m][0], (2, 1, 3)[k])
            copies.append(remote(s1.at[m, rows_at(spot * QUARTER, QUARTER, QUARTER)], r1.at[m, k], *sems(m, 1), device))
        matrix_send(m, 1, copies)

    def stage_2(m):
        matrix_wait(m, 1)
        spot = me.at[AXES[m][0]]
        part = grads[m, rows_at(spot * QUARTER, QUARTER, QUARTER)]
        for k in range(3):
            part = part + r1[m, k].astype(F32)
        h2[m] = part
        s2[m] = part.astype(BF16)
        copies = []
        for k, (line, lane, device) in enumerate(me.plane(AXES[m][1:])):
            piece = s2.at[m, rows_at(line * SIXTEENTH, SIXTEENTH, SIXTEENTH), rows_at(lane * BLOCK, BLOCK, BLOCK)]
            copies.append(remote(piece, r2.at[m, k], *sems(m, 2), device))
        matrix_send(m, 2, copies)

    def block_of(m, depth):
        begin = mine
        if depth >= 1:
            begin = begin + me.at[AXES[m][0]] * QUARTER
        if depth >= 2:
            begin = begin + me.at[AXES[m][1]] * SIXTEENTH
        line = rows_at(begin, (HALF, QUARTER, SIXTEENTH)[depth], SIXTEENTH)
        if m == OUT:
            return sum_out.at[line]
        return sum_in.at[m % 3, line]

    def stage_3(m):
        matrix_wait(m, 2)
        lane = rows_at(me.at[AXES[m][2]] * BLOCK, BLOCK, BLOCK)
        part = h2[m, rows_at(me.at[AXES[m][1]] * SIXTEENTH, SIXTEENTH, SIXTEENTH), lane]
        for k in range(15):
            part = part + r2[m, k].astype(F32)
        block = block_of(m, 2).at[:, lane]
        block[...] = part.astype(BF16)
        peers = me.plane(AXES[m][1:])
        matrix_send(m, 3, [remote(block, block, *sems(m, 3), peers[k][2]) for k in range(15)])

    def stage_4(m):
        matrix_wait(m, 3)
        block = block_of(m, 1)
        matrix_send(m, 4, [remote(block, block, *sems(m, 4), me.other(AXES[m][0], (2, 1, 3)[k])[1]) for k in range(3)])

    def stage_5(m):
        matrix_wait(m, 4)
        block = block_of(m, 0)
        matrix_send(m, 5, [remote(block, block, *sems(m, 5), me.partner)])

    def stage_6(m):
        matrix_wait(m, 5)

    zero = jnp.zeros((8, D), F32)
    sums = (zero, zero)
    for c in range(n_chunks):
        sums = forward(c, sums)
    gain_rows, out_rows = sums
    out_part = lambda at: acc_out[pl.ds(at, HALF)] + dot(act[CHUNK:, pl.ds(at, HALF)], d_mix[CHUNK:], (0, 0))
    gradient_theirs(OUT, out_part)
    gradient_mine(OUT, out_part)
    in_rows = zero
    for c in range(n_chunks):
        if comm and c == 1:
            stage_1(OUT)
        in_rows = backward(c, in_rows)

    line = lax.broadcasted_iota(jnp.int32, (8, D), 0)
    total = jnp.zeros((8, D), F32)
    for k, part in enumerate((in_rows, out_rows, gain_rows)):
        part = jnp.sum(part, axis=0, keepdims=True)
        total = jnp.where(line == k, part / gain_row if k == 2 else part, total)
    if comm:
        v_core[me.core] = total
        vector_send("core")
    else:
        vectors[...] = total

    final = pl.ds(EDGE - CHUNK, CHUNK)
    q[...] = dot(onehot_t[...], d_pre[...]).astype(BF16)
    parts = {
        SENDERS_IN: lambda at: dot(ext[:, pl.ds(at, HALF)], q[:EXT], (0, 0)),
        RECEIVERS_IN: lambda at: dot(ext[:NODE, pl.ds(at, HALF)], q[EXT:], (0, 0)),
        EDGES_IN: lambda at: dot(edge[:, pl.ds(at, HALF)], d_pre[...], (0, 0)),
    }
    for m in (SENDERS_IN, RECEIVERS_IN):
        gradient_theirs(m, parts[m])
    for m in (SENDERS_IN, RECEIVERS_IN):
        gradient_mine(m, parts[m])
    back_out[...] = dot(q[NODE:EXT], w_in[D : 2 * D], (1, 1)).astype(BF16)
    back_to = (me.west, me.east, me.south, me.north)
    back_copies = [
        remote(back_out.at[pl.ds(k * HALO, HALO)], back.at[pl.ds(k * HALO, HALO)], halo_send.at[1], halo_recv.at[1], back_to[k])
        for k in range(4)
    ]
    if comm:
        for copy in back_copies:
            copy.start()
    else:
        back[...] = back_out[...]
    gradient_theirs(EDGES_IN, parts[EDGES_IN])
    if comm:
        stage_1(SENDERS_IN)
        stage_1(RECEIVERS_IN)
    gradient_mine(EDGES_IN, parts[EDGES_IN])
    if comm:
        stage_1(EDGES_IN)
        v_axes[0, me.lat] = vector_sum("core")
        vector_send("x")
    own_table[...] = dot(q[:NODE], w_in[D : 2 * D], (1, 1)) + dot(q[EXT:], w_in[2 * D :], (1, 1))

    def last(c, _):
        here = rows_at(c * CHUNK, CHUNK, CHUNK)
        live = lax.broadcasted_iota(jnp.int32, (CHUNK, 1), 0) + c * CHUNK < count[0]
        d_edge = dot(d_pre[here], w_in[:D], (1, 1))
        edge_grad[here] = jnp.where(live, cot[here].astype(F32) + d_edge, 0.0).astype(BF16)
        return 0

    lax.fori_loop(0, n_chunks, last, 0)

    if comm:
        pl.semaphore_wait(plane_sem, 9)
        for m in range(4):
            stage_2(m)
        v_axes[1, me.y] = vector_sum("x")
        vector_send("y")
        arrived(back, halo_recv.at[1])
    back_in = (None, None, (me.lat < 3).astype(BF16), (me.lat > 0).astype(BF16))
    for k in range(4):
        if back_in[k] is not None:
            back[k * HALO : (k + 1) * HALO] = back[k * HALO : (k + 1) * HALO] * back_in[k]
    node_grad[...] = (own_table[...] + dot(list_t[...], back[...])).astype(BF16)

    if comm:
        for m in range(4):
            stage_3(m)
        v_axes[2, me.z] = vector_sum("y")
        vector_send("z")
        for m in range(4):
            stage_4(m)
        vectors[...] = vector_sum("z")
        for m in range(4):
            stage_5(m)
        for m in range(4):
            stage_6(m)
        arrived(rows, halo_send.at[0])
        arrived(back_out, halo_send.at[1])
        arrived(v_core.at[0], v_send.at[0])
        for n in range(3):
            arrived(v_axes.at[n, pl.ds(0, 3)], v_send.at[1 + n])
        for m in range(4):
            for stage in range(6):
                arrived(like(m, stage), m_send.at[m, stage])


def call(comm, *args):
    vmem = pl.BlockSpec(memory_space=pltpu.VMEM)
    hbm = pl.BlockSpec(memory_space=pltpu.HBM)
    V = pltpu.VMEM
    dma = pltpu.SemaphoreType.DMA
    return pl.pallas_call(
        functools.partial(kernel, comm),
        out_shape=(
            V((EDGE, D), BF16), V((NODE, D), BF16), V((D, D), BF16), V((3, D, D), BF16), V((8, D), F32),
        ),
        in_specs=[hbm] * 13,
        out_specs=(vmem, vmem, vmem, vmem, vmem),
        scratch_shapes=[
            pltpu.SMEM((1,), jnp.int32), V((1, 4, HALO), jnp.int32), V((EDGE // BLOCK, BLOCK), jnp.int32), V((EDGE // BLOCK, BLOCK), jnp.int32),
            V((1, D), F32), V((1, D), F32), V((1, D), F32),
            V((EXT, D), BF16), V((EDGE, D), BF16), V((EDGE, D), BF16), V((3 * D, D), BF16), V((D, D), BF16),
            V((NODE, D), BF16), dma((13,)),
            V((4 * HALO, D), BF16), V((4 * HALO, D), BF16), V((4 * HALO, D), BF16), V((4 * HALO, D), BF16),
            dma((2,)), dma((2,)),
            V((EDGE, TABLE), BF16), V((TABLE, EDGE), BF16), V((NODE, 4 * HALO), BF16), V((TABLE, D), BF16),
            V((EDGE, D), F32), V((EDGE, D), BF16), V((2, CHUNK, D), F32), V((2, CHUNK, D), F32), V((2, CHUNK, D), F32), V((2, CHUNK, D), F32),
            V((D, D), F32), V((TABLE, D), F32),
            V((EDGE, D), BF16), V((EDGE, D), BF16),
            V((TABLE, D), BF16), V((NODE, D), F32),
            V((4, HALF, D), F32), V((4, HALF, D), BF16), V((4, HALF, D), BF16), V((4, HALF, D), BF16),
            V((4, 3, QUARTER, D), BF16), V((4, QUARTER, D), F32), V((4, QUARTER, D), BF16),
            V((4, 15, SIXTEENTH, BLOCK), BF16), dma((4, 6)), dma((4, 6)),
            V((2, 8, D), F32), V((3, 4, 8, D), F32), dma((4,)), dma((4,)), pltpu.SemaphoreType.REGULAR,
        ],
        compiler_params=pltpu.CompilerParams(
            collective_id=0 if comm else None, has_side_effects=True, vmem_limit_bytes=57 * 2**20
        ),
    )(*args)


def finish_kernel(
    edge_grad, node_grad, sum_out, sum_in, vectors,
    edge_grad_hbm, node_grad_hbm, w_in_hbm, b_in_out, w_out_hbm, b_out_out, gain_out,
    wide, sem,
):
    copies = [
        pltpu.make_async_copy(edge_grad, edge_grad_hbm, sem.at[0]),
        pltpu.make_async_copy(node_grad, node_grad_hbm, sem.at[1]),
        pltpu.make_async_copy(vectors.at[pl.ds(0, 1)], b_in_out, sem.at[6]),
        pltpu.make_async_copy(vectors.at[pl.ds(1, 1)], b_out_out, sem.at[7]),
        pltpu.make_async_copy(vectors.at[pl.ds(2, 1)], gain_out, sem.at[8]),
    ]
    for copy in copies:
        copy.start()
    for m in range(4):
        wide[m] = (sum_in[m] if m < 3 else sum_out[...]).astype(F32)
        to = w_in_hbm.at[pl.ds(m * D, D)] if m < 3 else w_out_hbm
        copies.append(pltpu.make_async_copy(wide.at[m], to, sem.at[2 + m]))
        copies[-1].start()
    for copy in copies:
        copy.wait()


def finish(*args):
    vmem = pl.BlockSpec(memory_space=pltpu.VMEM)
    hbm = pl.BlockSpec(memory_space=pltpu.HBM)
    vector = jax.ShapeDtypeStruct((1, D), F32)
    return pl.pallas_call(
        finish_kernel,
        out_shape=(
            jax.ShapeDtypeStruct((EDGE, D), BF16), jax.ShapeDtypeStruct((NODE, D), BF16),
            jax.ShapeDtypeStruct((3 * D, D), F32), vector, jax.ShapeDtypeStruct((D, D), F32), vector, vector,
        ),
        in_specs=[vmem] * 5,
        out_specs=(hbm,) * 7,
        scratch_shapes=[pltpu.VMEM((4, D, D), F32), pltpu.SemaphoreType.DMA((9,))],
        compiler_params=pltpu.CompilerParams(vmem_limit_bytes=12 * 2**20),
    )(*args)


def body(
    node_latent, edge_latent, edge_sender, edge_receiver, edge_count, halo_send,
    weight_in, bias_in, weight_out, bias_out, norm_gain, edge_cotangent, node_cotangent, comm=True,
):
    results = call(
        comm,
        node_latent, edge_latent, edge_sender.reshape(EDGE // BLOCK, BLOCK), edge_receiver.reshape(EDGE // BLOCK, BLOCK),
        edge_count, halo_send, weight_in, bias_in.reshape(1, D), weight_out, bias_out.reshape(1, D),
        norm_gain.reshape(1, D), edge_cotangent, node_cotangent,
    )
    edge_grad, node_grad, w_in, b_in, w_out, b_out, gain = finish(*results)
    return edge_grad, node_grad, w_in, b_in.reshape(D), w_out, b_out.reshape(D), gain.reshape(D)


def solution(mesh):
    both = P(("lon", "lat"))
    rows = P(("lon", "lat"), None)
    return jax.shard_map(
        body,
        mesh=mesh,
        in_specs=(rows, rows, both, both, both, P(("lon", "lat"), None, None), P(), P(), P(), P(), P(), rows, rows),
        out_specs=(rows, rows, P(), P(), P(), P(), P()),
        check_vma=False,
    )
```
